512 devices in a mesh: dp: 8 (over z), tile: 64 (over x, y, core).
Axes of the slice: x: 4, y: 8, z: 8, core: 2. Of those that a mesh axis runs over, the one named last changes fastest.
Arguments:
- features: bfloat16 [8, 64, 16, 16, 256], P('dp', 'tile'), may hold values from -6 to 6
- cotangent: bfloat16 [8, 64, 16, 16, 256], P('dp', 'tile'), may hold values from -6 to 6
- weight: bfloat16 [3, 3, 256, 256], replicated, may hold values from -0.125 to 0.125
- tile_owner: int32 [8, 64], P('dp'), may hold values from 0 to 63, as said below
- tile_neighbors: int32 [8, 64, 8], P('dp'), may hold values from -1 to 63, as said below
- tile_counts: int32 [8], P('dp'), may hold values from 32 to 64, as said below
Outputs:
- out_features: bfloat16 [8, 64, 16, 16, 256], P('dp', 'tile')
- grad_features: bfloat16 [8, 64, 16, 16, 256], P('dp', 'tile')
- grad_weight: bfloat16 [3, 3, 256, 256], replicated
The draws below stay inside these ranges and needn't reach their ends.
Inputs may be any that keep to these rules, and one draw needn't show every extreme that they name: `tile_owner`: each slide's row is a permutation of the devices 0 to 63. `tile_neighbors`: entries name list positions below the slide's count, each tile's neighbors are distinct and the relation is symmetric (opposite directions); list positions at or above the count have only -1. `tile_counts`: slide 0 has all 64 slots live.
All inputs are finite; a program needn't handle non-finite values.
Results may differ from the reference program's by a relative error of at most 0.001.
Values may be sent and summed in bfloat16 or wider, within the bound.
No kernel may reach another device: no remote copies, remote signals or barrier semaphores. Data moves between devices by JAX's collectives and lax.ppermute only.
A program may use at most 64 MiB of HBM per device.

```python
import math
import jax
import jax.numpy as jnp
from jax import lax

CHANNEL_COUNT = 256
TILE_SIDE_CELLS = 16
DILATION_SPAN = 4
SLIDES = 8
TILES = 64


row_span = 8


def tile_layout(key):
    key_count, key_perm, key_shift = jax.random.split(key, 3)
    counts = jax.random.randint(key_count, (SLIDES,), TILES // 2, TILES + 1)
    counts = jnp.where(jnp.arange(SLIDES) == 0, TILES, counts).astype(jnp.int32)
    owners = jax.vmap(lambda k: jax.random.permutation(k, TILES))(jax.random.split(key_perm, SLIDES)).astype(jnp.int32)
    row_total = (TILES + row_span - 1) // row_span
    row_shift = jax.random.randint(key_shift, (SLIDES, row_total), 0, 3)
    positions = jnp.arange(TILES, dtype=jnp.int32)
    row_index = positions // row_span
    col_index = positions % row_span + jnp.take(row_shift, row_index, axis=1)
    offsets_row = jnp.array([-1, -1, -1, 0, 0, 1, 1, 1], jnp.int32)
    offsets_col = jnp.array([-1, 0, 1, -1, 1, -1, 0, 1], jnp.int32)
    want_row = row_index[None, :, None] + offsets_row[None, None, :]
    want_col = col_index[:, :, None] + offsets_col[None, None, :]
    valid_pos = positions[None, :] < counts[:, None]
    matches = (row_index[None, None, None, :] == want_row[..., None]) & (col_index[:, None, None, :] == want_col[..., None]) & valid_pos[:, None, None, :]
    has_match = jnp.any(matches, axis=-1) & valid_pos[:, :, None]
    found_pos = jnp.sum(jnp.where(matches, positions[None, None, None, :], 0), axis=-1)
    neighbors = jnp.where(has_match, found_pos, -1).astype(jnp.int32)
    return (owners, neighbors, counts)


def draw_tile_owner(key, part):
    return tile_layout(key)[0]


def draw_tile_neighbors(key, part):
    return tile_layout(key)[1]


def draw_tile_counts(key, part):
    return tile_layout(key)[2]


def block_levels(stream_key, dims, cuts, least, largest):
    factor_of = 1.0
    for position, blocks in cuts:
        heights = jax.random.uniform(jax.random.fold_in(jax.random.fold_in(stream_key, 6), position), (blocks,), jnp.float32, least / len(cuts), largest / len(cuts))
        factor_of = factor_of * jnp.repeat(jnp.exp(heights), dims[position] // blocks).reshape((-1,) + (1,) * (len(dims) - 1 - position))
    return factor_of


def centred(key, dims, scale, limit, cuts=(), kind=jnp.bfloat16):
    level = block_levels(key, dims, cuts, -0.22, 0.18) if cuts else 1.0
    values = jax.random.normal(key, dims, jnp.float32) * scale * level
    return jnp.minimum(jnp.maximum(values, -limit), limit).astype(kind)


def setup_inputs(seed: int = 0) -> dict:
    keys = jax.random.split(jax.random.key(seed), 7)
    return {
        "features": centred(keys[0], (SLIDES, TILES, TILE_SIDE_CELLS, TILE_SIDE_CELLS, CHANNEL_COUNT), 1.0, 6.0, ((0, 8), (1, 64))),
        "cotangent": centred(keys[1], (SLIDES, TILES, TILE_SIDE_CELLS, TILE_SIDE_CELLS, CHANNEL_COUNT), 1.0, 6.0, ((0, 8), (1, 64))),
        "weight": centred(keys[2], (3, 3, CHANNEL_COUNT, CHANNEL_COUNT), (9 * CHANNEL_COUNT) ** -0.5, 0.125),
        "tile_owner": draw_tile_owner(jax.random.fold_in(keys[6], 71), 0),
        "tile_neighbors": draw_tile_neighbors(jax.random.fold_in(keys[6], 71), 0),
        "tile_counts": draw_tile_counts(jax.random.fold_in(keys[6], 71), 0),
    }


def peer_table(tile_owner, tile_neighbors, tile_counts):
    positions = jnp.arange(TILES, dtype=jnp.int32)
    held = lax.optimization_barrier(jnp.sum(jnp.where(tile_owner[:, :, None] == positions[None, None, :], positions[None, :, None], 0), axis=1)).astype(jnp.int32)
    is_live = held < tile_counts[:, None]
    near_pos = jnp.take_along_axis(tile_neighbors, jnp.broadcast_to(held[:, :, None], (SLIDES, TILES, 8)), axis=1)
    near_dev = jnp.take_along_axis(tile_owner, jnp.maximum(near_pos, 0).reshape(SLIDES, TILES * 8), axis=1).reshape(SLIDES, TILES, 8)
    peer_dev = jnp.where(near_pos >= 0, near_dev, -1).astype(jnp.int32)
    return (is_live, peer_dev)

def surround(feature_field, device, peers):
    empty = jnp.zeros(feature_field.shape[1:], feature_field.dtype)
    pieces = [jnp.where(peers[d] >= 0, feature_field[jnp.maximum(peers[d], 0)], empty) for d in range(8)]
    top_band = jnp.concatenate(pieces[0:3], axis=1)
    middle_band = jnp.concatenate([pieces[3], feature_field[device], pieces[4]], axis=1)
    bottom_band = jnp.concatenate(pieces[5:8], axis=1)
    block_lattice = jnp.concatenate([top_band, middle_band, bottom_band], axis=0)
    return block_lattice[TILE_SIDE_CELLS - DILATION_SPAN:2 * TILE_SIDE_CELLS + DILATION_SPAN, TILE_SIDE_CELLS - DILATION_SPAN:2 * TILE_SIDE_CELLS + DILATION_SPAN]

def forward_taps(padded_tile, weight):
    summed = jnp.zeros((TILE_SIDE_CELLS * TILE_SIDE_CELLS, CHANNEL_COUNT), jnp.float32)
    for first_operand in range(3):
        for second_operand in range(3):
            sliding_window = padded_tile[DILATION_SPAN * first_operand:DILATION_SPAN * first_operand + TILE_SIDE_CELLS, DILATION_SPAN * second_operand:DILATION_SPAN * second_operand + TILE_SIDE_CELLS].reshape(TILE_SIDE_CELLS * TILE_SIDE_CELLS, CHANNEL_COUNT)
            summed = summed + jnp.dot(sliding_window, weight[first_operand, second_operand], preferred_element_type=jnp.float32)
    return summed.reshape(TILE_SIDE_CELLS, TILE_SIDE_CELLS, CHANNEL_COUNT)

def backward_taps(padded_tile, weight):
    summed = jnp.zeros((TILE_SIDE_CELLS * TILE_SIDE_CELLS, CHANNEL_COUNT), jnp.float32)
    for first_operand in range(3):
        for second_operand in range(3):
            row_begin = 2 * DILATION_SPAN - DILATION_SPAN * first_operand
            column_begin = 2 * DILATION_SPAN - DILATION_SPAN * second_operand
            sliding_window = padded_tile[row_begin:row_begin + TILE_SIDE_CELLS, column_begin:column_begin + TILE_SIDE_CELLS].reshape(TILE_SIDE_CELLS * TILE_SIDE_CELLS, CHANNEL_COUNT)
            summed = summed + jnp.dot(sliding_window, weight[first_operand, second_operand].T, preferred_element_type=jnp.float32)
    return summed.reshape(TILE_SIDE_CELLS, TILE_SIDE_CELLS, CHANNEL_COUNT)

def weight_taps(padded_tile, grad_rows):
    result = []
    for first_operand in range(3):
        row_list = []
        for second_operand in range(3):
            sliding_window = padded_tile[DILATION_SPAN * first_operand:DILATION_SPAN * first_operand + TILE_SIDE_CELLS, DILATION_SPAN * second_operand:DILATION_SPAN * second_operand + TILE_SIDE_CELLS].reshape(TILE_SIDE_CELLS * TILE_SIDE_CELLS, CHANNEL_COUNT)
            row_list.append(jnp.dot(sliding_window.T, grad_rows, preferred_element_type=jnp.float32))
        result.append(jnp.stack(row_list))
    return jnp.stack(result)

def reference(features, cotangent, weight, tile_owner, tile_neighbors, tile_counts):
    is_live, peer_dev = peer_table(tile_owner, tile_neighbors, tile_counts)
    mask = is_live[:, :, None, None, None]
    masked_x = jnp.where(mask, features, jnp.zeros_like(features))
    masked_g = jnp.where(mask, cotangent, jnp.zeros_like(cotangent))

    def one_tile(running, index):
        slide = index // TILES
        device = index % TILES
        peers = peer_dev[slide, device]
        keep = is_live[slide, device]
        padded_x = surround(masked_x[slide], device, peers)
        padded_g = surround(masked_g[slide], device, peers)
        out_tile = jnp.where(keep, forward_taps(padded_x, weight), 0.0).astype(jnp.bfloat16)
        grad_tile = jnp.where(keep, backward_taps(padded_g, weight), 0.0).astype(jnp.bfloat16)
        grad_rows = masked_g[slide, device].reshape(TILE_SIDE_CELLS * TILE_SIDE_CELLS, CHANNEL_COUNT)
        running = running + weight_taps(padded_x, grad_rows)
        return (running, (out_tile, grad_tile))
    start = jnp.zeros((3, 3, CHANNEL_COUNT, CHANNEL_COUNT), jnp.float32)
    summed, (out_tiles, grad_tiles) = lax.scan(one_tile, start, jnp.arange(SLIDES * TILES, dtype=jnp.int32))
    grad_scale = 1.0 / math.sqrt(SLIDES * TILES * TILE_SIDE_CELLS * TILE_SIDE_CELLS)
    out_features = out_tiles.reshape(features.shape)
    grad_features = grad_tiles.reshape(features.shape)
    grad_weight = (summed * grad_scale).astype(jnp.bfloat16)
    return (out_features, grad_features, grad_weight)
```

```python
import functools
import math

import jax
import jax.numpy as jnp
from jax import lax
from jax.experimental import pallas as pl
from jax.experimental.pallas import tpu as pltpu
from jax.sharding import PartitionSpec as P

SPAN = 4
CELLS = SPAN * SPAN
CLASSES = SPAN * SPAN
PAD = SPAN + 2
HALF = 128
QUARTER = 64
bf16, f32 = jnp.bfloat16, jnp.float32


def device_of(m, hi, ho):
    return m * 4 + ho * 2 + hi


def vmem(n):
    return [pl.BlockSpec(memory_space=pltpu.VMEM)] * n


PARAMS = pltpu.CompilerParams(vmem_limit_bytes=24 * 1024 * 1024)


def live_mask(owner, device, count):
    positions = lax.broadcasted_iota(jnp.int32, owner.shape, 1)
    held = jnp.sum(jnp.where(owner == device, positions, 0).astype(f32), axis=1, keepdims=True)
    return held < count.astype(f32)


def class_order(transposed):
    n = CLASSES * CELLS
    o = lax.broadcasted_iota(jnp.int32, (n, n), 1 if transposed else 0)
    c = lax.broadcasted_iota(jnp.int32, (n, n), 0 if transposed else 1)
    mr, mc, r, k = o >> 6, (o >> 4) & 3, (o >> 2) & 3, o & 3
    return c == (r * SPAN + mr) * 16 + k * SPAN + mc


def swap16():
    o = lax.broadcasted_iota(jnp.int32, (256, 256), 0)
    c = lax.broadcasted_iota(jnp.int32, (256, 256), 1)
    return jnp.where(c == ((o & 15) << 4) + (o >> 4), 1.0, 0.0).astype(bf16)


def dot(a, b):
    return jnp.dot(a, b, preferred_element_type=f32)


def split_kernel(place_ref, x_ref, g_ref, owner_ref, send_ref):
    live = live_mask(owner_ref[...], place_ref[0], place_ref[1])
    order = jnp.where(class_order(False) & live, 1.0, 0.0).astype(bf16)
    x = dot(order, x_ref[...]).astype(bf16)
    g = dot(order, g_ref[...]).astype(bf16)
    for m in range(CLASSES):
        for hi in range(2):
            for ho in range(2):
                rows = slice(m * CELLS, (m + 1) * CELLS)
                j = device_of(m, hi, ho)
                send_ref[j, :, :HALF] = x[rows, hi * HALF : (hi + 1) * HALF]
                send_ref[j, :, HALF:] = g[rows, ho * HALF : (ho + 1) * HALF]


def surround(padded, cells, sel_ref):
    def put(d, sources, targets):
        width = cells[0].shape[1]
        got = dot(sel_ref[d], jnp.concatenate([cells[s] for s in sources], axis=1)).astype(bf16)
        for n, (r, c) in enumerate(targets):
            padded[r * PAD + c] = got[:, n * width : (n + 1) * width]

    for r in range(SPAN):
        for c in range(SPAN):
            padded[(r + 1) * PAD + c + 1] = cells[r * SPAN + c]
    last, side = SPAN - 1, range(SPAN)
    put(0, [last * SPAN + last], [(0, 0)])
    put(1, [last * SPAN + c for c in side], [(0, c + 1) for c in side])
    put(2, [last * SPAN], [(0, PAD - 1)])
    put(3, [r * SPAN + last for r in side], [(r + 1, 0) for r in side])
    put(4, [r * SPAN for r in side], [(r + 1, PAD - 1) for r in side])
    put(5, [last], [(PAD - 1, 0)])
    put(6, [c for c in side], [(PAD - 1, c + 1) for c in side])
    put(7, [0], [(PAD - 1, PAD - 1)])


def window(padded, a, b):
    rows = [padded[(r + a) * PAD + c + b] for r in range(SPAN) for c in range(SPAN)]
    return jnp.concatenate(rows, axis=0)


def weight_kernel(recv_ref, sel_ref, sum_ref, x_ref, g_ref, padded):
    swap = swap16()
    for k in range(recv_ref.shape[0] // 16):
        rows = recv_ref[k * 16 : (k + 1) * 16].reshape(256, 2 * HALF)
        turned = dot(swap, rows).astype(bf16)
        for s in range(CELLS):
            x_ref[s, k * 16 : (k + 1) * 16, :] = turned[s * 16 : (s + 1) * 16, :HALF]
            g_ref[s, k * 16 : (k + 1) * 16, :] = turned[s * 16 : (s + 1) * 16, HALF:]
    surround(padded, [x_ref[s] for s in range(CELLS)], sel_ref)
    grad = g_ref[...].reshape(-1, HALF).T
    for a in range(3):
        for b in range(3):
            tap = a * 3 + b
            sum_ref[tap * HALF : (tap + 1) * HALF, :] = dot(grad, window(padded, a, b)).T


def conv_kernel(xa_ref, xb_ref, ga_ref, gb_ref, sel_ref, wo_ref, wg_ref, out_ref, padded):
    def taps(a_ref, b_ref, w_ref, flip):
        surround(padded, [jnp.concatenate([a_ref[s], b_ref[s]], axis=1) for s in range(CELLS)], sel_ref)
        total = jnp.zeros((CELLS * a_ref.shape[1], QUARTER), f32)
        for a in range(3):
            for b in range(3):
                view = window(padded, 2 - a, 2 - b) if flip else window(padded, a, b)
                total = total + dot(view, w_ref[a * 3 + b])
        return total

    forward = taps(xa_ref, xb_ref, wo_ref, False)
    backward = taps(ga_ref, gb_ref, wg_ref, True)
    both = jnp.concatenate([forward, backward], axis=1).astype(bf16)
    tiles = xa_ref.shape[1]
    swap = swap16()
    for k in range(tiles // 16):
        rows = [both[s * tiles + k * 16 : s * tiles + (k + 1) * 16] for s in range(CELLS)]
        turned = dot(swap, jnp.concatenate(rows, axis=0)).astype(bf16)
        out_ref[k * 16 : (k + 1) * 16] = turned.reshape(16, CELLS, 2 * QUARTER)


def join_kernel(place_ref, recv_ref, owner_ref, out_ref, grad_ref):
    live = live_mask(owner_ref[...], place_ref[0], place_ref[1])
    order = jnp.where(class_order(True) & live, 1.0, 0.0).astype(bf16)

    def join(low):
        rows = []
        for m in range(CLASSES):
            parts = [recv_ref[device_of(m, hi, ho), :, low : low + QUARTER] for hi in range(2) for ho in range(2)]
            rows.append(jnp.concatenate(parts, axis=1))
        return dot(order, jnp.concatenate(rows, axis=0)).astype(bf16)

    out_ref[...] = join(0)
    grad_ref[...] = join(QUARTER)


def neighbour_table(owner, neighbors):
    tiles = owner.shape[0]
    positions = jnp.arange(tiles, dtype=jnp.int32)
    beside = jnp.sum(jnp.where(neighbors[:, :, None] == positions, owner + 1, 0), axis=2) - 1
    peer = jnp.sum(jnp.where((owner == positions[:, None])[:, :, None], beside[None], 0), axis=1)
    return (peer.T[:, :, None] == positions).astype(bf16)


def local(features, cotangent, weight, tile_owner, tile_neighbors, tile_counts):
    tiles = lax.axis_size("tile")
    slides = lax.axis_size("dp")
    device = lax.axis_index("tile")
    hi, ho = device % 2, (device // 2) % 2
    width = features.shape[-1]
    cells = features.shape[2] * features.shape[3]
    place = jnp.stack([device, tile_counts[0]])
    smem = pl.BlockSpec(memory_space=pltpu.SMEM)

    send = pl.pallas_call(
        split_kernel,
        out_shape=jax.ShapeDtypeStruct((tiles, CELLS, 2 * HALF), bf16),
        in_specs=[smem, *vmem(3)],
        out_specs=vmem(1)[0],
        compiler_params=PARAMS,
        name="split",
    )(place, features.reshape(cells, width), cotangent.reshape(cells, width), tile_owner)
    recv = lax.all_to_all(send, "tile", 0, 0, tiled=True)

    sel = neighbour_table(tile_owner[0], tile_neighbors[0])
    taps = weight.shape[0] * weight.shape[1]
    block = (CELLS, tiles, HALF)
    partial, x_own, g_own = pl.pallas_call(
        weight_kernel,
        out_shape=[
            jax.ShapeDtypeStruct((taps * HALF, HALF), f32),
            jax.ShapeDtypeStruct(block, bf16),
            jax.ShapeDtypeStruct(block, bf16),
        ],
        in_specs=vmem(2),
        out_specs=vmem(3),
        scratch_shapes=[pltpu.VMEM((PAD * PAD, tiles, HALF), bf16)],
        compiler_params=PARAMS,
        name="weight_taps",
    )(recv, sel)

    groups = [[device_of(m, i, o) for m in range(CLASSES)] for o in range(2) for i in range(2)]
    rows = taps * HALF // CLASSES
    parts = lax.all_to_all(
        partial.reshape(CLASSES, rows, HALF), "tile", 0, 0, tiled=True, axis_index_groups=groups
    )
    part = jnp.sum(parts, axis=0)
    parts = lax.all_to_all(jnp.broadcast_to(part, (slides, rows, HALF)), "dp", 0, 0, tiled=True)
    scale = 1.0 / math.sqrt(slides * tiles * cells)
    part = (jnp.sum(parts, axis=0) * scale).astype(bf16)
    groups = [[device_of(m, i, o) for o in range(2) for m in range(CLASSES)] for i in range(2)]
    mine = lax.all_to_all(
        jnp.broadcast_to(part, (2 * CLASSES, rows, HALF)), "tile", 0, 0, tiled=True, axis_index_groups=groups
    )
    core = [(j, j ^ 1) for j in range(tiles)]
    other = lax.ppermute(mine, "tile", core)
    low = jnp.where(hi == 0, mine, other)
    high = jnp.where(hi == 0, other, mine)

    def whole_rows(half):
        return half.reshape(2, taps, HALF, HALF).transpose(1, 2, 0, 3).reshape(taps, HALF, 2 * HALF)

    grad_weight = jnp.concatenate([whole_rows(low), whole_rows(high)], axis=1).reshape(weight.shape)

    x_other = lax.ppermute(x_own, "tile", core)
    g_other = lax.ppermute(g_own, "tile", [(j, j ^ 2) for j in range(tiles)])
    quarter = (2 * hi + ho) * QUARTER
    flat = weight.reshape(taps, width, width)

    def half_first(array, half):
        swapped = jnp.concatenate([array[:, HALF:], array[:, :HALF]], axis=1)
        return jnp.where(half == 0, array, swapped)

    w_out = half_first(lax.dynamic_slice_in_dim(flat, quarter, QUARTER, axis=2), hi)
    w_grad = half_first(lax.dynamic_slice_in_dim(flat, quarter, QUARTER, axis=1).transpose(0, 2, 1), ho)
    back = pl.pallas_call(
        conv_kernel,
        out_shape=jax.ShapeDtypeStruct((tiles, CELLS, 2 * QUARTER), bf16),
        in_specs=vmem(7),
        out_specs=vmem(1)[0],
        scratch_shapes=[pltpu.VMEM((PAD * PAD, tiles, 2 * HALF), bf16)],
        compiler_params=PARAMS,
        name="conv_taps",
    )(x_own, x_other, g_own, g_other, sel, w_out, w_grad)
    back = lax.all_to_all(back, "tile", 0, 0, tiled=True)
    out, grad = pl.pallas_call(
        join_kernel,
        out_shape=[jax.ShapeDtypeStruct((cells, width), bf16)] * 2,
        in_specs=[smem, *vmem(2)],
        out_specs=vmem(2),
        compiler_params=PARAMS,
        name="join",
    )(place, back, tile_owner)
    return out.reshape(features.shape), grad.reshape(features.shape), grad_weight


def solution(mesh):
    return jax.shard_map(
        local,
        mesh=mesh,
        in_specs=(
            P("dp", "tile", None, None, None),
            P("dp", "tile", None, None, None),
            P(),
            P("dp", None),
            P("dp", None, None),
            P("dp"),
        ),
        out_specs=(P("dp", "tile", None, None, None), P("dp", "tile", None, None, None), P()),
        check_vma=False,
    )
```

```python
import functools
import math

import jax
import jax.numpy as jnp
from jax import lax
from jax.experimental import pallas as pl
from jax.experimental.pallas import tpu as pltpu
from jax.sharding import PartitionSpec as P

SPAN = 4
CELLS = SPAN * SPAN
CLASSES = SPAN * SPAN
PAD = SPAN + 2
HALF = 128
QUARTER = 64
ROWS = 8
COLUMNS = 4
BACK_ROWS = COLUMNS * 2 * CELLS
PIECE_ROWS = 80
bf16, f32 = jnp.bfloat16, jnp.float32


def device_of(m, hi, ho):
    return ho * 32 + m * 2 + hi


def vmem(n):
    return [pl.BlockSpec(memory_space=pltpu.VMEM)] * n


PARAMS = pltpu.CompilerParams(vmem_limit_bytes=24 * 1024 * 1024)


def live_mask(owner, device, count):
    positions = lax.broadcasted_iota(jnp.int32, owner.shape, 1)
    held = jnp.sum(jnp.where(owner == device, positions, 0).astype(f32), axis=1, keepdims=True)
    return held < count.astype(f32)


def class_order(transposed):
    n = CLASSES * CELLS
    o = lax.broadcasted_iota(jnp.int32, (n, n), 1 if transposed else 0)
    c = lax.broadcasted_iota(jnp.int32, (n, n), 0 if transposed else 1)
    mr, mc, r, k = o >> 6, (o >> 4) & 3, (o >> 2) & 3, o & 3
    return c == (r * SPAN + mr) * 16 + k * SPAN + mc


def swap16():
    o = lax.broadcasted_iota(jnp.int32, (256, 256), 0)
    c = lax.broadcasted_iota(jnp.int32, (256, 256), 1)
    return jnp.where(c == ((o & 15) << 4) + (o >> 4), 1.0, 0.0).astype(bf16)


def dot(a, b):
    return jnp.dot(a, b, preferred_element_type=f32)


def split_kernel(place_ref, owner_hbm, x_hbm, g_hbm, send_ref, owner_ref, x_ref, g_ref, sems):
    pairs = [(owner_hbm, owner_ref), (x_hbm, x_ref), (g_hbm, g_ref)]
    copies = [pltpu.make_async_copy(src, dst, sems.at[n]) for n, (src, dst) in enumerate(pairs)]
    for copy in copies:
        copy.start()
    order = class_order(False)
    for copy in copies:
        copy.wait()
    live = live_mask(owner_ref[...], place_ref[0], place_ref[1])
    order = jnp.where(order & live, 1.0, 0.0).astype(bf16)
    x = dot(order, x_ref[...]).astype(bf16)
    g = dot(order, g_ref[...]).astype(bf16)
    for m in range(CLASSES):
        rows = slice(m * CELLS, (m + 1) * CELLS)
        for ho in range(2):
            chip = device_of(m, 0, ho) // 2
            send_ref[chip, :, : 2 * HALF] = x[rows]
            send_ref[chip, :, 2 * HALF :] = g[rows]


def surround(padded, cells, sel_ref):
    def put(d, sources, targets):
        width = cells[0].shape[1]
        got = dot(sel_ref[d], jnp.concatenate([cells[s] for s in sources], axis=1)).astype(bf16)
        for n, (r, c) in enumerate(targets):
            padded[r * PAD + c] = got[:, n * width : (n + 1) * width]

    for r in range(SPAN):
        for c in range(SPAN):
            padded[(r + 1) * PAD + c + 1] = cells[r * SPAN + c]
    last, side = SPAN - 1, range(SPAN)
    put(0, [last * SPAN + last], [(0, 0)])
    put(1, [last * SPAN + c for c in side], [(0, c + 1) for c in side])
    put(2, [last * SPAN], [(0, PAD - 1)])
    put(3, [r * SPAN + last for r in side], [(r + 1, 0) for r in side])
    put(4, [r * SPAN for r in side], [(r + 1, PAD - 1) for r in side])
    put(5, [last], [(PAD - 1, 0)])
    put(6, [c for c in side], [(PAD - 1, c + 1) for c in side])
    put(7, [0], [(PAD - 1, PAD - 1)])


def window(padded, a, b):
    rows = [padded[(r + a) * PAD + c + b] for r in range(SPAN) for c in range(SPAN)]
    return jnp.concatenate(rows, axis=0)


def weight_kernel(place_ref, own_ref, other_ref, sel_ref, sum_ref, x_ref, g_ref, padded):
    swap = swap16()
    chips = own_ref.shape[0]
    for n, ref in enumerate((own_ref, other_ref)):
        for k in range(0, chips, 16):
            turned = dot(swap, ref[k : k + 16].reshape(256, 4 * HALF)).astype(bf16)
            tiles = slice(n * chips + k, n * chips + k + 16)
            for s in range(CELLS):
                x_ref[s, tiles, :] = turned[s * 16 : (s + 1) * 16, : 2 * HALF]
                g_ref[s, tiles, :] = turned[s * 16 : (s + 1) * 16, 2 * HALF :]
    device = place_ref[0]
    low_x, low_g = device % 2 == 0, device < chips
    x = [jnp.where(low_x, x_ref[s, :, :HALF], x_ref[s, :, HALF:]) for s in range(CELLS)]
    surround(padded, x, sel_ref)
    grad = jnp.where(low_g, g_ref[:, :, :HALF], g_ref[:, :, HALF:]).reshape(-1, HALF).T
    for a in range(3):
        for b in range(3):
            tap = a * 3 + b
            sum_ref[tap * HALF : (tap + 1) * HALF, :] = dot(grad, window(padded, a, b)).T


def conv_kernel(place_ref, x_ref, g_ref, sel_ref, wo_ref, wg_ref, own_ref, other_ref, padded):
    tiles = x_ref.shape[1]

    def taps(cells_ref, w_ref, flip):
        surround(padded, [cells_ref[s] for s in range(CELLS)], sel_ref)
        total = jnp.zeros((CELLS * tiles, QUARTER), f32)
        for a in range(3):
            for b in range(3):
                view = window(padded, 2 - a, 2 - b) if flip else window(padded, a, b)
                total = total + dot(view, w_ref[a * 3 + b])
        return total

    forward = taps(x_ref, wo_ref, False)
    backward = taps(g_ref, wg_ref, True)
    both = jnp.concatenate([forward, backward], axis=1).astype(bf16)
    swap = swap16()
    column = place_ref[0] // (2 * ROWS)
    chips = tiles // 2
    for n, ref in enumerate((own_ref, other_ref)):
        for k in range(0, chips, 16):
            begin = n * chips + k
            rows = [both[s * tiles + begin : s * tiles + begin + 16] for s in range(CELLS)]
            turned = dot(swap, jnp.concatenate(rows, axis=0)).astype(bf16).reshape(16, CELLS, 2 * QUARTER)
            for half in range(16 // ROWS):
                there = (k // ROWS + half) ^ column
                ref[pl.ds(there, 1)] = turned[half * ROWS : (half + 1) * ROWS][None]


def pack_kernel(scale, back_ref, parts_ref, out_ref):
    total = parts_ref[0]
    for s in range(1, parts_ref.shape[0]):
        total = total + parts_ref[s]
    piece = (total * scale).astype(bf16)
    piece = jnp.concatenate([piece, jnp.zeros((PIECE_ROWS - piece.shape[0], HALF), bf16)], axis=0)
    for y in range(ROWS):
        for n in range(back_ref.shape[0]):
            for i in range(2):
                begin = (n * 2 + i) * CELLS
                out_ref[y, begin : begin + CELLS, :] = back_ref[n, i, y]
        out_ref[y, BACK_ROWS:, :] = piece


def join_kernel(place_ref, recv_ref, owner_ref, out_ref, grad_ref):
    live = live_mask(owner_ref[...], place_ref[0], place_ref[1])
    order = jnp.where(class_order(True) & live, 1.0, 0.0).astype(bf16)

    column, core = place_ref[0] // (2 * ROWS), place_ref[0] % 2
    classes = []
    for m in range(CLASSES):
        quarters = []
        for hi in range(2):
            for ho in range(2):
                chip = device_of(m, 0, ho) // 2
                slot = ((chip // ROWS) ^ column) * 2 + (hi ^ core)
                begin = pl.multiple_of(slot * CELLS, CELLS)
                quarters.append(recv_ref[chip % ROWS, pl.ds(begin, CELLS), :])
        classes.append(quarters)

    def join(low):
        rows = [jnp.concatenate([part[:, low : low + QUARTER] for part in parts], axis=1) for parts in classes]
        return dot(order, jnp.concatenate(rows, axis=0)).astype(bf16)

    out_ref[...] = join(0)
    grad_ref[...] = join(QUARTER)


def rows_kernel(place_ref, mine_ref, other_ref, out_ref):
    low = place_ref[0] % 2 == 0
    for tap in range(mine_ref.shape[1]):
        mine = jnp.concatenate([mine_ref[0, tap], mine_ref[1, tap]], axis=1)
        other = jnp.concatenate([other_ref[0, tap], other_ref[1, tap]], axis=1)
        out_ref[tap, :HALF, :] = jnp.where(low, mine, other)
        out_ref[tap, HALF:, :] = jnp.where(low, other, mine)


def neighbour_table(owner, neighbors, names):
    positions = jnp.arange(owner.shape[0], dtype=jnp.int32)
    beside = jnp.sum(jnp.where(neighbors[:, :, None] == positions, owner + 1, 0), axis=2) - 1
    peer = jnp.sum(jnp.where((owner == names[:, None])[:, :, None], beside[None], 0), axis=1)
    return (peer.T[:, :, None] == names).astype(bf16)


def local(features, cotangent, weight, tile_owner, tile_neighbors, tile_counts):
    tiles = lax.axis_size("tile")
    slides = lax.axis_size("dp")
    device = lax.axis_index("tile")
    hi, ho = device % 2, device // (tiles // 2)
    width = features.shape[-1]
    cells = features.shape[2] * features.shape[3]
    place = jnp.stack([device, tile_counts[0]])
    smem = pl.BlockSpec(memory_space=pltpu.SMEM)
    hbm = pl.BlockSpec(memory_space=pltpu.HBM)

    chips = tiles // 2
    core = [(j, j ^ 1) for j in range(tiles)]
    same_core = [[2 * c + i for c in range(chips)] for i in range(2)]
    send = pl.pallas_call(
        split_kernel,
        out_shape=jax.ShapeDtypeStruct((chips, CELLS, 4 * HALF), bf16),
        in_specs=[smem, hbm, hbm, hbm],
        out_specs=vmem(1)[0],
        scratch_shapes=[
            pltpu.VMEM((1, tiles), jnp.int32),
            pltpu.VMEM((cells, width), bf16),
            pltpu.VMEM((cells, width), bf16),
            pltpu.SemaphoreType.DMA((3,)),
        ],
        name="split",
    )(place, tile_owner, features.reshape(cells, width), cotangent.reshape(cells, width))
    own = lax.all_to_all(send, "tile", 0, 0, tiled=True, axis_index_groups=same_core)

    side = jnp.arange(chips, dtype=jnp.int32) * 2
    names = jnp.concatenate([side + hi, side + 1 - hi])
    sel = neighbour_table(tile_owner[0], tile_neighbors[0], names)
    taps = weight.shape[0] * weight.shape[1]
    quarter = (2 * hi + ho) * QUARTER
    flat = weight.reshape(taps, width, width)
    w_out = lax.dynamic_slice_in_dim(flat, quarter, QUARTER, axis=2)
    w_grad = lax.dynamic_slice_in_dim(flat, quarter, QUARTER, axis=1).transpose(0, 2, 1)
    own, sel, w_out, w_grad = lax.optimization_barrier((own, sel, w_out, w_grad))
    other = lax.ppermute(own, "tile", core)

    block = (CELLS, tiles, width)
    partial, x, g = pl.pallas_call(
        weight_kernel,
        out_shape=[
            jax.ShapeDtypeStruct((taps * HALF, HALF), f32),
            jax.ShapeDtypeStruct(block, bf16),
            jax.ShapeDtypeStruct(block, bf16),
        ],
        in_specs=[smem, *vmem(3)],
        out_specs=vmem(3),
        scratch_shapes=[pltpu.VMEM((PAD * PAD, tiles, HALF), bf16)],
        compiler_params=PARAMS,
        name="weight_taps",
    )(place, own, other, sel)

    groups = [[device_of(m, i, o) for m in range(CLASSES)] for o in range(2) for i in range(2)]
    rows = taps * HALF // CLASSES
    parts = lax.all_to_all(
        partial.reshape(CLASSES, rows, HALF), "tile", 0, 0, tiled=True, axis_index_groups=groups
    )
    outgoing = jax.ShapeDtypeStruct((COLUMNS, ROWS, CELLS, 2 * QUARTER), bf16)
    back_own, back_other = pl.pallas_call(
        conv_kernel,
        out_shape=[outgoing, outgoing],
        in_specs=[smem, *vmem(5)],
        out_specs=vmem(2),
        scratch_shapes=[pltpu.VMEM((PAD * PAD, tiles, width), bf16)],
        compiler_params=PARAMS,
        name="conv_taps",
    )(place, x, g, sel, w_out, w_grad)
    back_other = lax.ppermute(back_other, "tile", core)
    back = jnp.stack([back_own, back_other], axis=1)
    turned = [back[0]]
    for n in range(1, COLUMNS):
        turned.append(lax.ppermute(back[n], "tile", [(j, j ^ (n * 2 * ROWS)) for j in range(tiles)]))
    back = jnp.stack(turned)
    parts, back = lax.optimization_barrier((parts, back))

    part = jnp.sum(parts, axis=0)
    parts = lax.all_to_all(jnp.broadcast_to(part, (slides, rows, HALF)), "dp", 0, 0, tiled=True)
    scale = 1.0 / math.sqrt(slides * tiles * cells)
    along_y = [[(x * ROWS + y) * 2 + i for y in range(ROWS)] for x in range(COLUMNS) for i in range(2)]
    along_x = [[(x * ROWS + y) * 2 + i for x in range(COLUMNS)] for y in range(ROWS) for i in range(2)]
    packed = pl.pallas_call(
        functools.partial(pack_kernel, scale),
        out_shape=jax.ShapeDtypeStruct((ROWS, BACK_ROWS + PIECE_ROWS, HALF), bf16),
        in_specs=vmem(2),
        out_specs=vmem(1)[0],
        compiler_params=PARAMS,
        name="pack",
    )(back, parts)
    packed = lax.all_to_all(packed, "tile", 0, 0, tiled=True, axis_index_groups=along_y)
    column = packed[:, BACK_ROWS : BACK_ROWS + rows]
    mine = lax.all_to_all(
        jnp.broadcast_to(column, (COLUMNS, ROWS, rows, HALF)), "tile", 0, 0, tiled=True, axis_index_groups=along_x
    )
    other = lax.ppermute(mine, "tile", core)
    halves = (2, taps, HALF, HALF)
    grad_weight = pl.pallas_call(
        rows_kernel,
        out_shape=jax.ShapeDtypeStruct((taps, width, width), bf16),
        in_specs=[smem, *vmem(2)],
        out_specs=vmem(1)[0],
        compiler_params=PARAMS,
        name="rows",
    )(place, mine.reshape(halves), other.reshape(halves)).reshape(weight.shape)

    out, grad = pl.pallas_call(
        join_kernel,
        out_shape=[jax.ShapeDtypeStruct((cells, width), bf16)] * 2,
        in_specs=[smem, *vmem(2)],
        out_specs=vmem(2),
        compiler_params=PARAMS,
        name="join",
    )(place, packed, tile_owner)
    return out.reshape(features.shape), grad.reshape(features.shape), grad_weight


def solution(mesh):
    return jax.shard_map(
        local,
        mesh=mesh,
        in_specs=(
            P("dp", "tile", None, None, None),
            P("dp", "tile", None, None, None),
            P(),
            P("dp", None),
            P("dp", None, None),
            P("dp"),
        ),
        out_specs=(P("dp", "tile", None, None, None), P("dp", "tile", None, None, None), P()),
        check_vma=False,
    )
```

```python
import functools
import math

import jax
import jax.numpy as jnp
from jax import lax
from jax.experimental import pallas as pl
from jax.experimental.pallas import tpu as pltpu
from jax.sharding import PartitionSpec as P

SPAN = 4
CELLS = SPAN * SPAN
CLASSES = SPAN * SPAN
PAD = SPAN + 2
HALF = 128
QUARTER = 64
ROWS = 8
COLUMNS = 4
PIECE_ROWS = 80
bf16, f32 = jnp.bfloat16, jnp.float32


def device_of(m, hi, ho):
    return ho * 32 + m * 2 + hi


def vmem(n):
    return [pl.BlockSpec(memory_space=pltpu.VMEM)] * n


PARAMS = pltpu.CompilerParams(vmem_limit_bytes=24 * 1024 * 1024)


def live_mask(owner, count):
    device = lax.axis_index("tile")
    positions = lax.broadcasted_iota(jnp.int32, owner.shape, 1)
    held = jnp.sum(jnp.where(owner == device, positions, 0).astype(f32), axis=1, keepdims=True)
    return held < count.astype(f32)


def class_order(transposed):
    n = CLASSES * CELLS
    o = lax.broadcasted_iota(jnp.int32, (n, n), 1 if transposed else 0)
    c = lax.broadcasted_iota(jnp.int32, (n, n), 0 if transposed else 1)
    mr, mc, r, k = o >> 6, (o >> 4) & 3, (o >> 2) & 3, o & 3
    return c == (r * SPAN + mr) * 16 + k * SPAN + mc


def swap16():
    o = lax.broadcasted_iota(jnp.int32, (256, 256), 0)
    c = lax.broadcasted_iota(jnp.int32, (256, 256), 1)
    return jnp.where(c == ((o & 15) << 4) + (o >> 4), 1.0, 0.0).astype(bf16)


def dot(a, b):
    return jnp.dot(a, b, preferred_element_type=f32)


def split_kernel(count_ref, owner_hbm, x_hbm, g_hbm, send_ref, owner_ref, x_ref, g_ref, sems):
    pairs = [(owner_hbm, owner_ref), (x_hbm, x_ref), (g_hbm, g_ref)]
    copies = [pltpu.make_async_copy(src, dst, sems.at[n]) for n, (src, dst) in enumerate(pairs)]
    for copy in copies:
        copy.start()
    order = class_order(False)
    for copy in copies:
        copy.wait()
    live = live_mask(owner_ref[...], count_ref[0])
    order = jnp.where(order & live, 1.0, 0.0).astype(bf16)
    x = dot(order, x_ref[...]).astype(bf16)
    g = dot(order, g_ref[...]).astype(bf16)
    for m in range(CLASSES):
        rows = slice(m * CELLS, (m + 1) * CELLS)
        for ho in range(2):
            chip = device_of(m, 0, ho) // 2
            send_ref[chip, :, : 2 * HALF] = x[rows]
            send_ref[chip, :, 2 * HALF :] = g[rows]


def surround(padded, cells, sel_ref):
    def put(d, sources, targets):
        width = cells[0].shape[1]
        got = dot(sel_ref[d], jnp.concatenate([cells[s] for s in sources], axis=1)).astype(bf16)
        for n, (r, c) in enumerate(targets):
            padded[r * PAD + c] = got[:, n * width : (n + 1) * width]

    for r in range(SPAN):
        for c in range(SPAN):
            padded[(r + 1) * PAD + c + 1] = cells[r * SPAN + c]
    last, side = SPAN - 1, range(SPAN)
    put(0, [last * SPAN + last], [(0, 0)])
    put(1, [last * SPAN + c for c in side], [(0, c + 1) for c in side])
    put(2, [last * SPAN], [(0, PAD - 1)])
    put(3, [r * SPAN + last for r in side], [(r + 1, 0) for r in side])
    put(4, [r * SPAN for r in side], [(r + 1, PAD - 1) for r in side])
    put(5, [last], [(PAD - 1, 0)])
    put(6, [c for c in side], [(PAD - 1, c + 1) for c in side])
    put(7, [0], [(PAD - 1, PAD - 1)])


def window(padded, a, b):
    rows = [padded[(r + a) * PAD + c + b] for r in range(SPAN) for c in range(SPAN)]
    return jnp.concatenate(rows, axis=0)


def by_cell(refs, put, lanes):
    swap = swap16()
    chips = refs[0].shape[0]
    for n, ref in enumerate(refs):
        for k in range(0, chips, 16):
            turned = dot(swap, lanes(ref, k).reshape(256, -1)).astype(bf16)
            for s in range(CELLS):
                put(s, slice(n * chips + k, n * chips + k + 16), turned[s * 16 : (s + 1) * 16])


def weight_kernel(own_ref, other_ref, sel_ref, sum_ref, x_ref, g_ref, padded):
    device = lax.axis_index("tile")
    low_x, low_g = device % 2 == 0, device < own_ref.shape[0]

    def halves(ref, k):
        rows = ref[k : k + 16]
        x = jnp.where(low_x, rows[:, :, :HALF], rows[:, :, HALF : 2 * HALF])
        g = jnp.where(low_g, rows[:, :, 2 * HALF : 3 * HALF], rows[:, :, 3 * HALF :])
        return jnp.concatenate([x, g], axis=2)

    def put(s, tiles, value):
        x_ref[s, tiles, :] = value[:, :HALF]
        g_ref[s, tiles, :] = value[:, HALF:]

    by_cell((own_ref, other_ref), put, halves)
    surround(padded, [x_ref[s] for s in range(CELLS)], sel_ref)
    grad = g_ref[...].reshape(-1, HALF).T
    for a in range(3):
        for b in range(3):
            tap = a * 3 + b
            sum_ref[tap * HALF : (tap + 1) * HALF, :] = dot(grad, window(padded, a, b)).T


def conv_kernel(
    own_in_ref, other_in_ref, sel_ref, wo_ref, wg_ref, own_ref, other_ref, x_ref, g_ref, padded
):
    tiles = x_ref.shape[1]
    width = x_ref.shape[2]

    def put(s, where, value):
        x_ref[s, where, :] = value[:, :width]
        g_ref[s, where, :] = value[:, width:]

    by_cell((own_in_ref, other_in_ref), put, lambda ref, k: ref[k : k + 16])

    def taps(cells_ref, w_ref, flip):
        surround(padded, [cells_ref[s] for s in range(CELLS)], sel_ref)
        total = jnp.zeros((CELLS * tiles, QUARTER), f32)
        for a in range(3):
            for b in range(3):
                view = window(padded, 2 - a, 2 - b) if flip else window(padded, a, b)
                total = total + dot(view, w_ref[a * 3 + b])
        return total

    forward = taps(x_ref, wo_ref, False)
    backward = taps(g_ref, wg_ref, True)
    both = jnp.concatenate([forward, backward], axis=1).astype(bf16)
    swap = swap16()
    chips = tiles // 2
    for n, ref in enumerate((own_ref, other_ref)):
        for k in range(0, chips, 16):
            begin = n * chips + k
            rows = [both[s * tiles + begin : s * tiles + begin + 16] for s in range(CELLS)]
            turned = dot(swap, jnp.concatenate(rows, axis=0)).astype(bf16)
            ref[k : k + 16] = turned.reshape(16, CELLS, 2 * QUARTER)


def pack_y_kernel(scale, own_ref, other_ref, parts_ref, out_ref):
    total = parts_ref[0]
    for s in range(1, parts_ref.shape[0]):
        total = total + parts_ref[s]
    piece = (total * scale).astype(bf16)
    piece = jnp.concatenate([piece, jnp.zeros((PIECE_ROWS - piece.shape[0], HALF), bf16)], axis=0)
    for y in range(ROWS):
        for x in range(COLUMNS):
            for i, ref in enumerate((own_ref, other_ref)):
                begin = (x * 2 + i) * CELLS
                out_ref[y, begin : begin + CELLS, :] = ref[x * ROWS + y]
        out_ref[y, COLUMNS * 2 * CELLS :, :] = piece


def pack_x_kernel(size, in_ref, out_ref):
    pair = 2 * CELLS
    pieces = [in_ref[y, COLUMNS * pair :, :].astype(f32)[:size] for y in range(ROWS)]
    pieces = jnp.concatenate(pieces, axis=0).astype(bf16)
    for x in range(COLUMNS):
        for y in range(ROWS):
            out_ref[x, y * pair : (y + 1) * pair, :] = in_ref[y, x * pair : (x + 1) * pair, :]
        out_ref[x, ROWS * pair :, :] = pieces


def join_kernel(count_ref, recv_ref, owner_ref, out_ref, grad_ref):
    live = live_mask(owner_ref[...], count_ref[0])
    order = jnp.where(class_order(True) & live, 1.0, 0.0).astype(bf16)

    core = lax.axis_index("tile") % 2
    classes = []
    for m in range(CLASSES):
        quarters = []
        for hi in range(2):
            for ho in range(2):
                chip = device_of(m, 0, ho) // 2
                begin = pl.multiple_of((chip % ROWS * 2 + (hi ^ core)) * CELLS, CELLS)
                quarters.append(recv_ref[chip // ROWS, pl.ds(begin, CELLS), :])
        classes.append(quarters)

    def join(low):
        rows = [jnp.concatenate([part[:, low : low + QUARTER] for part in parts], axis=1) for parts in classes]
        return dot(order, jnp.concatenate(rows, axis=0)).astype(bf16)

    out_ref[...] = join(0)
    grad_ref[...] = join(QUARTER)


def rows_kernel(mine_ref, other_ref, out_ref):
    low = lax.axis_index("tile") % 2 == 0
    begin = ROWS * 2 * CELLS

    def half(ref, ho):
        return jnp.concatenate([ref[ho * 2, begin:, :], ref[ho * 2 + 1, begin:, :]], axis=0)

    for ho in range(2):
        mine, other = half(mine_ref, ho), half(other_ref, ho)
        columns = slice(ho * HALF, (ho + 1) * HALF)
        for tap in range(out_ref.shape[0]):
            rows = slice(tap * HALF, (tap + 1) * HALF)
            out_ref[tap, :HALF, columns] = jnp.where(low, mine[rows], other[rows])
            out_ref[tap, HALF:, columns] = jnp.where(low, other[rows], mine[rows])


def neighbour_table(owner, neighbors, names):
    positions = jnp.arange(owner.shape[0], dtype=jnp.int32)
    beside = jnp.sum(jnp.where(neighbors[:, :, None] == positions, owner + 1, 0), axis=2) - 1
    peer = jnp.sum(jnp.where((owner == names[:, None])[:, :, None], beside[None], 0), axis=1)
    return (peer.T[:, :, None] == names).astype(bf16)


def local(features, cotangent, weight, tile_owner, tile_neighbors, tile_counts):
    tiles = lax.axis_size("tile")
    slides = lax.axis_size("dp")
    device = lax.axis_index("tile")
    hi, ho = device % 2, device // (tiles // 2)
    width = features.shape[-1]
    cells = features.shape[2] * features.shape[3]
    smem = pl.BlockSpec(memory_space=pltpu.SMEM)
    hbm = pl.BlockSpec(memory_space=pltpu.HBM)

    chips = tiles // 2
    core = [(j, j ^ 1) for j in range(tiles)]
    same_core = [[2 * c + i for c in range(chips)] for i in range(2)]
    send = pl.pallas_call(
        split_kernel,
        out_shape=jax.ShapeDtypeStruct((chips, CELLS, 4 * HALF), bf16),
        in_specs=[smem, hbm, hbm, hbm],
        out_specs=vmem(1)[0],
        scratch_shapes=[
            pltpu.VMEM((1, tiles), jnp.int32),
            pltpu.VMEM((cells, width), bf16),
            pltpu.VMEM((cells, width), bf16),
            pltpu.SemaphoreType.DMA((3,)),
        ],
        name="split",
    )(tile_counts, tile_owner, features.reshape(cells, width), cotangent.reshape(cells, width))
    own = lax.all_to_all(send, "tile", 0, 0, tiled=True, axis_index_groups=same_core)

    side = jnp.arange(chips, dtype=jnp.int32) * 2
    names = jnp.concatenate([side + hi, side + 1 - hi])
    sel = neighbour_table(tile_owner[0], tile_neighbors[0], names)
    taps = weight.shape[0] * weight.shape[1]
    quarter = (2 * hi + ho) * QUARTER
    flat = weight.reshape(taps, width, width)
    w_out = lax.dynamic_slice_in_dim(flat, quarter, QUARTER, axis=2)
    w_grad = lax.dynamic_slice_in_dim(flat, quarter, QUARTER, axis=1).transpose(0, 2, 1)
    own, sel, w_out, w_grad = lax.optimization_barrier((own, sel, w_out, w_grad))
    other = lax.ppermute(own, "tile", core)

    partial = pl.pallas_call(
        weight_kernel,
        out_shape=jax.ShapeDtypeStruct((taps * HALF, HALF), f32),
        in_specs=vmem(3),
        out_specs=vmem(1)[0],
        scratch_shapes=[pltpu.VMEM((n, tiles, HALF), bf16) for n in (CELLS, CELLS, PAD * PAD)],
        compiler_params=PARAMS,
        name="weight_taps",
    )(own, other, sel)

    groups = [[device_of(m, i, o) for m in range(CLASSES)] for o in range(2) for i in range(2)]
    rows = taps * HALF // CLASSES
    parts = lax.all_to_all(
        partial.reshape(CLASSES, rows, HALF), "tile", 0, 0, tiled=True, axis_index_groups=groups
    )
    outgoing = jax.ShapeDtypeStruct((chips, CELLS, 2 * QUARTER), bf16)
    back_own, back_other = pl.pallas_call(
        conv_kernel,
        out_shape=[outgoing, outgoing],
        in_specs=vmem(5),
        out_specs=vmem(2),
        scratch_shapes=[pltpu.VMEM((n, tiles, width), bf16) for n in (CELLS, CELLS, PAD * PAD)],
        compiler_params=PARAMS,
        name="conv_taps",
    )(own, other, sel, w_out, w_grad)
    back_other = lax.ppermute(back_other, "tile", core)
    parts, back_own, back_other = lax.optimization_barrier((parts, back_own, back_other))

    part = jnp.sum(parts, axis=0)
    parts = lax.all_to_all(jnp.broadcast_to(part, (slides, rows, HALF)), "dp", 0, 0, tiled=True)
    scale = 1.0 / math.sqrt(slides * tiles * cells)
    along_y = [[(x * ROWS + y) * 2 + i for y in range(ROWS)] for x in range(COLUMNS) for i in range(2)]
    along_x = [[(x * ROWS + y) * 2 + i for x in range(COLUMNS)] for y in range(ROWS) for i in range(2)]
    packed = pl.pallas_call(
        functools.partial(pack_y_kernel, scale),
        out_shape=jax.ShapeDtypeStruct((ROWS, COLUMNS * 2 * CELLS + PIECE_ROWS, HALF), bf16),
        in_specs=vmem(3),
        out_specs=vmem(1)[0],
        compiler_params=PARAMS,
        name="pack_y",
    )(back_own, back_other, parts)
    packed = lax.all_to_all(packed, "tile", 0, 0, tiled=True, axis_index_groups=along_y)
    packed = pl.pallas_call(
        functools.partial(pack_x_kernel, rows),
        out_shape=jax.ShapeDtypeStruct((COLUMNS, ROWS * (2 * CELLS + rows), HALF), bf16),
        in_specs=vmem(1),
        out_specs=vmem(1)[0],
        compiler_params=PARAMS,
        name="pack_x",
    )(packed)
    mine = lax.all_to_all(packed, "tile", 0, 0, tiled=True, axis_index_groups=along_x)
    other = lax.ppermute(mine, "tile", core)
    grad_weight = pl.pallas_call(
        rows_kernel,
        out_shape=jax.ShapeDtypeStruct((taps, width, width), bf16),
        in_specs=vmem(2),
        out_specs=vmem(1)[0],
        compiler_params=PARAMS,
        name="rows",
    )(mine, other).reshape(weight.shape)

    out, grad = pl.pallas_call(
        join_kernel,
        out_shape=[jax.ShapeDtypeStruct((cells, width), bf16)] * 2,
        in_specs=[smem, *vmem(2)],
        out_specs=vmem(2),
        compiler_params=PARAMS,
        name="join",
    )(tile_counts, mine, tile_owner)
    return out.reshape(features.shape), grad.reshape(features.shape), grad_weight


def solution(mesh):
    return jax.shard_map(
        local,
        mesh=mesh,
        in_specs=(
            P("dp", "tile", None, None, None),
            P("dp", "tile", None, None, None),
            P(),
            P("dp", None),
            P("dp", None, None),
            P("dp"),
        ),
        out_specs=(P("dp", "tile", None, None, None), P("dp", "tile", None, None, None), P()),
        check_vma=False,
    )
```

```python
import functools
import math

import jax
import jax.numpy as jnp
from jax import lax
from jax.experimental import pallas as pl
from jax.experimental.pallas import tpu as pltpu
from jax.sharding import PartitionSpec as P

SPAN = 4
CELLS = SPAN * SPAN
CLASSES = SPAN * SPAN
PAD = SPAN + 2
HALF = 128
QUARTER = 64
bf16, f32 = jnp.bfloat16, jnp.float32


def device_of(m, hi, ho):
    return ho * 32 + m * 2 + hi


def vmem(n):
    return [pl.BlockSpec(memory_space=pltpu.VMEM)] * n


PARAMS = pltpu.CompilerParams(vmem_limit_bytes=24 * 1024 * 1024)


def live_mask(owner, count):
    device = lax.axis_index("tile")
    positions = lax.broadcasted_iota(jnp.int32, owner.shape, 1)
    held = jnp.sum(jnp.where(owner == device, positions, 0).astype(f32), axis=1, keepdims=True)
    return held < count.astype(f32)


def class_order(transposed):
    n = CLASSES * CELLS
    o = lax.broadcasted_iota(jnp.int32, (n, n), 1 if transposed else 0)
    c = lax.broadcasted_iota(jnp.int32, (n, n), 0 if transposed else 1)
    mr, mc, r, k = o >> 6, (o >> 4) & 3, (o >> 2) & 3, o & 3
    return c == (r * SPAN + mr) * 16 + k * SPAN + mc


def swap16():
    o = lax.broadcasted_iota(jnp.int32, (256, 256), 0)
    c = lax.broadcasted_iota(jnp.int32, (256, 256), 1)
    return jnp.where(c == ((o & 15) << 4) + (o >> 4), 1.0, 0.0).astype(bf16)


def dot(a, b):
    return jnp.dot(a, b, preferred_element_type=f32)


def split_kernel(count_ref, owner_hbm, x_hbm, g_hbm, send_ref, owner_ref, x_ref, g_ref, sems):
    pairs = [(owner_hbm, owner_ref), (x_hbm, x_ref), (g_hbm, g_ref)]
    copies = [pltpu.make_async_copy(src, dst, sems.at[n]) for n, (src, dst) in enumerate(pairs)]
    for copy in copies:
        copy.start()
    order = class_order(False)
    for copy in copies:
        copy.wait()
    live = live_mask(owner_ref[...], count_ref[0])
    order = jnp.where(order & live, 1.0, 0.0).astype(bf16)
    x = dot(order, x_ref[...]).astype(bf16)
    g = dot(order, g_ref[...]).astype(bf16)
    for m in range(CLASSES):
        rows = slice(m * CELLS, (m + 1) * CELLS)
        for ho in range(2):
            chip = device_of(m, 0, ho) // 2
            send_ref[chip, :, : 2 * HALF] = x[rows]
            send_ref[chip, :, 2 * HALF :] = g[rows]


def surround(padded, cells, sel_ref):
    def put(d, sources, targets):
        width = cells[0].shape[1]
        got = dot(sel_ref[d], jnp.concatenate([cells[s] for s in sources], axis=1)).astype(bf16)
        for n, (r, c) in enumerate(targets):
            padded[r * PAD + c] = got[:, n * width : (n + 1) * width]

    for r in range(SPAN):
        for c in range(SPAN):
            padded[(r + 1) * PAD + c + 1] = cells[r * SPAN + c]
    last, side = SPAN - 1, range(SPAN)
    put(0, [last * SPAN + last], [(0, 0)])
    put(1, [last * SPAN + c for c in side], [(0, c + 1) for c in side])
    put(2, [last * SPAN], [(0, PAD - 1)])
    put(3, [r * SPAN + last for r in side], [(r + 1, 0) for r in side])
    put(4, [r * SPAN for r in side], [(r + 1, PAD - 1) for r in side])
    put(5, [last], [(PAD - 1, 0)])
    put(6, [c for c in side], [(PAD - 1, c + 1) for c in side])
    put(7, [0], [(PAD - 1, PAD - 1)])


def window(padded, a, b):
    rows = [padded[(r + a) * PAD + c + b] for r in range(SPAN) for c in range(SPAN)]
    return jnp.concatenate(rows, axis=0)


def by_cell(refs, put, lanes):
    swap = swap16()
    chips = refs[0].shape[0]
    for n, ref in enumerate(refs):
        for k in range(0, chips, 16):
            turned = dot(swap, lanes(ref, k).reshape(256, -1)).astype(bf16)
            for s in range(CELLS):
                put(s, slice(n * chips + k, n * chips + k + 16), turned[s * 16 : (s + 1) * 16])


def weight_kernel(own_ref, other_ref, sel_ref, sum_ref, x_ref, g_ref, padded):
    device = lax.axis_index("tile")
    low_x, low_g = device % 2 == 0, device < own_ref.shape[0]

    def halves(ref, k):
        rows = ref[k : k + 16]
        x = jnp.where(low_x, rows[:, :, :HALF], rows[:, :, HALF : 2 * HALF])
        g = jnp.where(low_g, rows[:, :, 2 * HALF : 3 * HALF], rows[:, :, 3 * HALF :])
        return jnp.concatenate([x, g], axis=2)

    def put(s, tiles, value):
        x_ref[s, tiles, :] = value[:, :HALF]
        g_ref[s, tiles, :] = value[:, HALF:]

    by_cell((own_ref, other_ref), put, halves)
    surround(padded, [x_ref[s] for s in range(CELLS)], sel_ref)
    grad = g_ref[...].reshape(-1, HALF).T
    for a in range(3):
        for b in range(3):
            tap = a * 3 + b
            sum_ref[tap * HALF : (tap + 1) * HALF, :] = dot(grad, window(padded, a, b)).T


def conv_kernel(
    own_in_ref, other_in_ref, sel_ref, wo_ref, wg_ref, own_ref, other_ref, x_ref, g_ref, padded
):
    tiles = x_ref.shape[1]
    width = x_ref.shape[2]

    def put(s, where, value):
        x_ref[s, where, :] = value[:, :width]
        g_ref[s, where, :] = value[:, width:]

    by_cell((own_in_ref, other_in_ref), put, lambda ref, k: ref[k : k + 16])

    def taps(cells_ref, w_ref, flip):
        surround(padded, [cells_ref[s] for s in range(CELLS)], sel_ref)
        total = jnp.zeros((CELLS * tiles, QUARTER), f32)
        for a in range(3):
            for b in range(3):
                view = window(padded, 2 - a, 2 - b) if flip else window(padded, a, b)
                total = total + dot(view, w_ref[a * 3 + b])
        return total

    forward = taps(x_ref, wo_ref, False)
    backward = taps(g_ref, wg_ref, True)
    both = jnp.concatenate([forward, backward], axis=1).astype(bf16)
    swap = swap16()
    chips = tiles // 2
    for n, ref in enumerate((own_ref, other_ref)):
        for k in range(0, chips, 16):
            begin = n * chips + k
            rows = [both[s * tiles + begin : s * tiles + begin + 16] for s in range(CELLS)]
            turned = dot(swap, jnp.concatenate(rows, axis=0)).astype(bf16)
            ref[k : k + 16] = turned.reshape(16, CELLS, 2 * QUARTER)


def pack_kernel(scale, own_ref, other_ref, parts_ref, out_ref):
    total = parts_ref[0]
    for s in range(1, parts_ref.shape[0]):
        total = total + parts_ref[s]
    piece = (total * scale).astype(bf16)
    for chip in range(out_ref.shape[0]):
        out_ref[chip, :CELLS, :] = own_ref[chip]
        out_ref[chip, CELLS : 2 * CELLS, :] = other_ref[chip]
        out_ref[chip, 2 * CELLS :, :] = piece


def join_kernel(count_ref, recv_ref, owner_ref, out_ref, grad_ref):
    live = live_mask(owner_ref[...], count_ref[0])
    order = jnp.where(class_order(True) & live, 1.0, 0.0).astype(bf16)

    core = lax.axis_index("tile") % 2
    classes = []
    for m in range(CLASSES):
        quarters = []
        for hi in range(2):
            for ho in range(2):
                chip = device_of(m, 0, ho) // 2
                begin = pl.multiple_of((hi ^ core) * CELLS, CELLS)
                quarters.append(recv_ref[chip, pl.ds(begin, CELLS), :])
        classes.append(quarters)

    def join(low):
        rows = [jnp.concatenate([part[:, low : low + QUARTER] for part in parts], axis=1) for parts in classes]
        return dot(order, jnp.concatenate(rows, axis=0)).astype(bf16)

    out_ref[...] = join(0)
    grad_ref[...] = join(QUARTER)


def rows_kernel(mine_ref, other_ref, out_ref):
    low = lax.axis_index("tile") % 2 == 0
    taps = out_ref.shape[0]

    def half(ref, ho):
        chips = [device_of(m, 0, ho) // 2 for m in range(CLASSES)]
        return jnp.concatenate([ref[c, 2 * CELLS :, :].astype(f32) for c in chips], axis=0)

    for ho in range(2):
        mine, other = half(mine_ref, ho), half(other_ref, ho)
        columns = slice(ho * HALF, (ho + 1) * HALF)
        for tap in range(taps):
            rows = slice(tap * HALF, (tap + 1) * HALF)
            out_ref[tap, :HALF, columns] = jnp.where(low, mine[rows], other[rows]).astype(bf16)
            out_ref[tap, HALF:, columns] = jnp.where(low, other[rows], mine[rows]).astype(bf16)


def neighbour_table(owner, neighbors, names):
    positions = jnp.arange(owner.shape[0], dtype=jnp.int32)
    beside = jnp.sum(jnp.where(neighbors[:, :, None] == positions, owner + 1, 0), axis=2) - 1
    peer = jnp.sum(jnp.where((owner == names[:, None])[:, :, None], beside[None], 0), axis=1)
    return (peer.T[:, :, None] == names).astype(bf16)


def local(features, cotangent, weight, tile_owner, tile_neighbors, tile_counts):
    tiles = lax.axis_size("tile")
    slides = lax.axis_size("dp")
    device = lax.axis_index("tile")
    hi, ho = device % 2, device // (tiles // 2)
    width = features.shape[-1]
    cells = features.shape[2] * features.shape[3]
    smem = pl.BlockSpec(memory_space=pltpu.SMEM)
    hbm = pl.BlockSpec(memory_space=pltpu.HBM)

    chips = tiles // 2
    core = [(j, j ^ 1) for j in range(tiles)]
    same_core = [[2 * c + i for c in range(chips)] for i in range(2)]
    send = pl.pallas_call(
        split_kernel,
        out_shape=jax.ShapeDtypeStruct((chips, CELLS, 4 * HALF), bf16),
        in_specs=[smem, hbm, hbm, hbm],
        out_specs=vmem(1)[0],
        scratch_shapes=[
            pltpu.VMEM((1, tiles), jnp.int32),
            pltpu.VMEM((cells, width), bf16),
            pltpu.VMEM((cells, width), bf16),
            pltpu.SemaphoreType.DMA((3,)),
        ],
        name="split",
    )(tile_counts, tile_owner, features.reshape(cells, width), cotangent.reshape(cells, width))
    own = lax.all_to_all(send, "tile", 0, 0, tiled=True, axis_index_groups=same_core)

    side = jnp.arange(chips, dtype=jnp.int32) * 2
    names = jnp.concatenate([side + hi, side + 1 - hi])
    sel = neighbour_table(tile_owner[0], tile_neighbors[0], names)
    taps = weight.shape[0] * weight.shape[1]
    quarter = (2 * hi + ho) * QUARTER
    flat = weight.reshape(taps, width, width)
    w_out = lax.dynamic_slice_in_dim(flat, quarter, QUARTER, axis=2)
    w_grad = lax.dynamic_slice_in_dim(flat, quarter, QUARTER, axis=1).transpose(0, 2, 1)
    own, sel, w_out, w_grad = lax.optimization_barrier((own, sel, w_out, w_grad))
    other = lax.ppermute(own, "tile", core)

    partial = pl.pallas_call(
        weight_kernel,
        out_shape=jax.ShapeDtypeStruct((taps * HALF, HALF), f32),
        in_specs=vmem(3),
        out_specs=vmem(1)[0],
        scratch_shapes=[pltpu.VMEM((n, tiles, HALF), bf16) for n in (CELLS, CELLS, PAD * PAD)],
        compiler_params=PARAMS,
        name="weight_taps",
    )(own, other, sel)

    groups = [[device_of(m, i, o) for m in range(CLASSES)] for o in range(2) for i in range(2)]
    rows = taps * HALF // CLASSES
    parts = lax.all_to_all(
        partial.reshape(CLASSES, rows, HALF), "tile", 0, 0, tiled=True, axis_index_groups=groups
    )
    outgoing = jax.ShapeDtypeStruct((chips, CELLS, 2 * QUARTER), bf16)
    back_own, back_other = pl.pallas_call(
        conv_kernel,
        out_shape=[outgoing, outgoing],
        in_specs=vmem(5),
        out_specs=vmem(2),
        scratch_shapes=[pltpu.VMEM((n, tiles, width), bf16) for n in (CELLS, CELLS, PAD * PAD)],
        compiler_params=PARAMS,
        name="conv_taps",
    )(own, other, sel, w_out, w_grad)
    back_other = lax.ppermute(back_other, "tile", core)
    parts, back_own, back_other = lax.optimization_barrier((parts, back_own, back_other))

    part = jnp.sum(parts, axis=0)
    parts = lax.all_to_all(jnp.broadcast_to(part, (slides, rows, HALF)), "dp", 0, 0, tiled=True)
    scale = 1.0 / math.sqrt(slides * tiles * cells)
    packed = pl.pallas_call(
        functools.partial(pack_kernel, scale),
        out_shape=jax.ShapeDtypeStruct((chips, 2 * CELLS + rows, HALF), bf16),
        in_specs=vmem(3),
        out_specs=vmem(1)[0],
        compiler_params=PARAMS,
        name="pack",
    )(back_own, back_other, parts)
    mine = lax.all_to_all(packed, "tile", 0, 0, tiled=True, axis_index_groups=same_core)
    other = lax.ppermute(mine, "tile", core)
    grad_weight = pl.pallas_call(
        rows_kernel,
        out_shape=jax.ShapeDtypeStruct((taps, width, width), bf16),
        in_specs=vmem(2),
        out_specs=vmem(1)[0],
        compiler_params=PARAMS,
        name="rows",
    )(mine, other).reshape(weight.shape)

    out, grad = pl.pallas_call(
        join_kernel,
        out_shape=[jax.ShapeDtypeStruct((cells, width), bf16)] * 2,
        in_specs=[smem, *vmem(2)],
        out_specs=vmem(2),
        compiler_params=PARAMS,
        name="join",
    )(tile_counts, mine, tile_owner)
    return out.reshape(features.shape), grad.reshape(features.shape), grad_weight


def solution(mesh):
    return jax.shard_map(
        local,
        mesh=mesh,
        in_specs=(
            P("dp", "tile", None, None, None),
            P("dp", "tile", None, None, None),
            P(),
            P("dp", None),
            P("dp", None, None),
            P("dp"),
        ),
        out_specs=(P("dp", "tile", None, None, None), P("dp", "tile", None, None, None), P()),
        check_vma=False,
    )
```

```python
import functools
import math

import jax
import jax.numpy as jnp
from jax import lax
from jax.experimental import pallas as pl
from jax.experimental.pallas import tpu as pltpu
from jax.sharding import PartitionSpec as P

SPAN = 4
CELLS = SPAN * SPAN
CLASSES = SPAN * SPAN
PAD = SPAN + 2
HALF = 128
QUARTER = 64
SHARE = 36
SHARE_ROWS = 40
bf16, f32 = jnp.bfloat16, jnp.float32


def device_of(m, hi, ho):
    return m // 4 * 16 + ho * 8 + m % 4 * 2 + hi


def vmem(n):
    return [pl.BlockSpec(memory_space=pltpu.VMEM)] * n


PARAMS = pltpu.CompilerParams(vmem_limit_bytes=24 * 1024 * 1024)


def live_mask(owner, count):
    device = lax.axis_index("tile")
    positions = lax.broadcasted_iota(jnp.int32, owner.shape, 1)
    held = jnp.sum(jnp.where(owner == device, positions, 0).astype(f32), axis=1, keepdims=True)
    return held < count.astype(f32)


def class_order(transposed):
    n = CLASSES * CELLS
    o = lax.broadcasted_iota(jnp.int32, (n, n), 1 if transposed else 0)
    c = lax.broadcasted_iota(jnp.int32, (n, n), 0 if transposed else 1)
    mr, mc, r, k = o >> 6, (o >> 4) & 3, (o >> 2) & 3, o & 3
    return c == (r * SPAN + mr) * 16 + k * SPAN + mc


def swap16():
    o = lax.broadcasted_iota(jnp.int32, (256, 256), 0)
    c = lax.broadcasted_iota(jnp.int32, (256, 256), 1)
    return jnp.where(c == ((o & 15) << 4) + (o >> 4), 1.0, 0.0).astype(bf16)


def dot(a, b):
    return jnp.dot(a, b, preferred_element_type=f32)


def split_kernel(count_ref, owner_hbm, x_hbm, g_hbm, send_ref, owner_ref, x_ref, g_ref, sems):
    pairs = [(owner_hbm, owner_ref), (x_hbm, x_ref), (g_hbm, g_ref)]
    copies = [pltpu.make_async_copy(src, dst, sems.at[n]) for n, (src, dst) in enumerate(pairs)]
    for copy in copies:
        copy.start()
    order = class_order(False)
    for copy in copies:
        copy.wait()
    live = live_mask(owner_ref[...], count_ref[0])
    order = jnp.where(order & live, 1.0, 0.0).astype(bf16)
    x = dot(order, x_ref[...]).astype(bf16)
    g = dot(order, g_ref[...]).astype(bf16)
    for m in range(CLASSES):
        rows = slice(m * CELLS, (m + 1) * CELLS)
        for ho in range(2):
            chip = device_of(m, 0, ho) // 2
            send_ref[chip, :, : 2 * HALF] = x[rows]
            send_ref[chip, :, 2 * HALF :] = g[rows]


def surround(padded, cells, sel_ref):
    def put(d, sources, targets):
        width = cells[0].shape[1]
        got = dot(sel_ref[d], jnp.concatenate([cells[s] for s in sources], axis=1)).astype(bf16)
        for n, (r, c) in enumerate(targets):
            padded[r * PAD + c] = got[:, n * width : (n + 1) * width]

    for r in range(SPAN):
        for c in range(SPAN):
            padded[(r + 1) * PAD + c + 1] = cells[r * SPAN + c]
    last, side = SPAN - 1, range(SPAN)
    put(0, [last * SPAN + last], [(0, 0)])
    put(1, [last * SPAN + c for c in side], [(0, c + 1) for c in side])
    put(2, [last * SPAN], [(0, PAD - 1)])
    put(3, [r * SPAN + last for r in side], [(r + 1, 0) for r in side])
    put(4, [r * SPAN for r in side], [(r + 1, PAD - 1) for r in side])
    put(5, [last], [(PAD - 1, 0)])
    put(6, [c for c in side], [(PAD - 1, c + 1) for c in side])
    put(7, [0], [(PAD - 1, PAD - 1)])


def window(padded, a, b):
    rows = [padded[(r + a) * PAD + c + b] for r in range(SPAN) for c in range(SPAN)]
    return jnp.concatenate(rows, axis=0)


def by_cell(refs, put, lanes):
    swap = swap16()
    chips = refs[0].shape[0]
    for n, ref in enumerate(refs):
        for k in range(0, chips, 16):
            turned = dot(swap, lanes(ref, k).reshape(256, -1)).astype(bf16)
            for s in range(CELLS):
                put(s, slice(n * chips + k, n * chips + k + 16), turned[s * 16 : (s + 1) * 16])


def share_of(m, parity):
    return m // 4 * 4 + m % 2 * 2 + parity, m // 2 % 2


def weight_kernel(own_ref, other_ref, sel_ref, out_ref, x_ref, g_ref, padded, sum_ref):
    device = lax.axis_index("tile")
    low_x, low_g = device % 2 == 0, device // 8 % 2 == 0

    def halves(ref, k):
        rows = ref[k : k + 16]
        x = jnp.where(low_x, rows[:, :, :HALF], rows[:, :, HALF : 2 * HALF])
        g = jnp.where(low_g, rows[:, :, 2 * HALF : 3 * HALF], rows[:, :, 3 * HALF :])
        return jnp.concatenate([x, g], axis=2)

    def put(s, tiles, value):
        x_ref[s, tiles, :] = value[:, :HALF]
        g_ref[s, tiles, :] = value[:, HALF:]

    by_cell((own_ref, other_ref), put, halves)
    surround(padded, [x_ref[s] for s in range(CELLS)], sel_ref)
    grad = g_ref[...].reshape(-1, HALF).T
    for a in range(3):
        for b in range(3):
            tap = a * 3 + b
            sum_ref[tap * HALF : (tap + 1) * HALF, :] = dot(grad, window(padded, a, b)).T
    fill = jnp.zeros((SHARE_ROWS - SHARE, HALF), f32)
    for m in range(CLASSES):
        for parity in range(2):
            piece, half = share_of(m, parity)
            begin = (m * 2 + parity) * SHARE
            out_ref[piece, half, :SHARE, :] = sum_ref[begin : begin + SHARE, :]
            out_ref[piece, half, SHARE:, :] = fill


def conv_kernel(
    own_in_ref, other_in_ref, sel_ref, wo_ref, wg_ref, own_ref, other_ref, x_ref, g_ref, padded
):
    tiles = x_ref.shape[1]
    width = x_ref.shape[2]

    def put(s, where, value):
        x_ref[s, where, :] = value[:, :width]
        g_ref[s, where, :] = value[:, width:]

    by_cell((own_in_ref, other_in_ref), put, lambda ref, k: ref[k : k + 16])

    def taps(cells_ref, w_ref, flip):
        surround(padded, [cells_ref[s] for s in range(CELLS)], sel_ref)
        total = jnp.zeros((CELLS * tiles, QUARTER), f32)
        for a in range(3):
            for b in range(3):
                view = window(padded, 2 - a, 2 - b) if flip else window(padded, a, b)
                total = total + dot(view, w_ref[a * 3 + b])
        return total

    forward = taps(x_ref, wo_ref, False)
    backward = taps(g_ref, wg_ref, True)
    both = jnp.concatenate([forward, backward], axis=1).astype(bf16)
    swap = swap16()
    chips = tiles // 2
    for n, ref in enumerate((own_ref, other_ref)):
        for k in range(0, chips, 16):
            begin = n * chips + k
            rows = [both[s * tiles + begin : s * tiles + begin + 16] for s in range(CELLS)]
            turned = dot(swap, jnp.concatenate(rows, axis=0)).astype(bf16)
            ref[k : k + 16] = turned.reshape(16, CELLS, 2 * QUARTER)


def pack_kernel(scale, own_ref, other_ref, parts_ref, out_ref, piece_ref):
    for parity in range(2):
        total = parts_ref[parity]
        for s in range(parity + 2, parts_ref.shape[0], 2):
            total = total + parts_ref[s]
        piece_ref[parity * SHARE : parity * SHARE + SHARE_ROWS, :] = total
    piece = (piece_ref[: 2 * SHARE, :] * scale).astype(bf16)
    for chip in range(out_ref.shape[0]):
        out_ref[chip, :CELLS, :] = own_ref[chip]
        out_ref[chip, CELLS : 2 * CELLS, :] = other_ref[chip]
        out_ref[chip, 2 * CELLS :, :] = piece


def join_kernel(count_ref, recv_ref, owner_ref, out_ref, grad_ref):
    live = live_mask(owner_ref[...], count_ref[0])
    order = jnp.where(class_order(True) & live, 1.0, 0.0).astype(bf16)

    core = lax.axis_index("tile") % 2
    classes = []
    for m in range(CLASSES):
        quarters = []
        for hi in range(2):
            for ho in range(2):
                chip = device_of(m, 0, ho) // 2
                begin = pl.multiple_of((hi ^ core) * CELLS, CELLS)
                quarters.append(recv_ref[chip, pl.ds(begin, CELLS), :])
        classes.append(quarters)

    def join(low):
        rows = [jnp.concatenate([part[:, low : low + QUARTER] for part in parts], axis=1) for parts in classes]
        return dot(order, jnp.concatenate(rows, axis=0)).astype(bf16)

    out_ref[...] = join(0)
    grad_ref[...] = join(QUARTER)


def rows_kernel(mine_ref, other_ref, out_ref):
    low = lax.axis_index("tile") % 2 == 0
    taps = out_ref.shape[0]

    def half(ref, ho):
        chips = [device_of(m, 0, ho) // 2 for m in range(CLASSES)]
        return jnp.concatenate([ref[c, 2 * CELLS :, :].astype(f32) for c in chips], axis=0)

    for ho in range(2):
        mine, other = half(mine_ref, ho), half(other_ref, ho)
        columns = slice(ho * HALF, (ho + 1) * HALF)
        for tap in range(taps):
            rows = slice(tap * HALF, (tap + 1) * HALF)
            out_ref[tap, :HALF, columns] = jnp.where(low, mine[rows], other[rows]).astype(bf16)
            out_ref[tap, HALF:, columns] = jnp.where(low, other[rows], mine[rows]).astype(bf16)


def neighbour_table(owner, neighbors, names):
    positions = jnp.arange(owner.shape[0], dtype=jnp.int32)
    beside = jnp.sum(jnp.where(neighbors[:, :, None] == positions, owner + 1, 0), axis=2) - 1
    peer = jnp.sum(jnp.where((owner == names[:, None])[:, :, None], beside[None], 0), axis=1)
    return (peer.T[:, :, None] == names).astype(bf16)


def local(features, cotangent, weight, tile_owner, tile_neighbors, tile_counts):
    tiles = lax.axis_size("tile")
    slides = lax.axis_size("dp")
    device = lax.axis_index("tile")
    hi, ho = device % 2, device // 8 % 2
    width = features.shape[-1]
    cells = features.shape[2] * features.shape[3]
    smem = pl.BlockSpec(memory_space=pltpu.SMEM)
    hbm = pl.BlockSpec(memory_space=pltpu.HBM)

    chips = tiles // 2
    core = [(j, j ^ 1) for j in range(tiles)]
    same_core = [[2 * c + i for c in range(chips)] for i in range(2)]
    send = pl.pallas_call(
        split_kernel,
        out_shape=jax.ShapeDtypeStruct((chips, CELLS, 4 * HALF), bf16),
        in_specs=[smem, hbm, hbm, hbm],
        out_specs=vmem(1)[0],
        scratch_shapes=[
            pltpu.VMEM((1, tiles), jnp.int32),
            pltpu.VMEM((cells, width), bf16),
            pltpu.VMEM((cells, width), bf16),
            pltpu.SemaphoreType.DMA((3,)),
        ],
        name="split",
    )(tile_counts, tile_owner, features.reshape(cells, width), cotangent.reshape(cells, width))
    own = lax.all_to_all(send, "tile", 0, 0, tiled=True, axis_index_groups=same_core)

    side = jnp.arange(chips, dtype=jnp.int32) * 2
    names = jnp.concatenate([side + hi, side + 1 - hi])
    sel = neighbour_table(tile_owner[0], tile_neighbors[0], names)
    taps = weight.shape[0] * weight.shape[1]
    quarter = (2 * hi + ho) * QUARTER
    flat = weight.reshape(taps, width, width)
    w_out = lax.dynamic_slice_in_dim(flat, quarter, QUARTER, axis=2)
    w_grad = lax.dynamic_slice_in_dim(flat, quarter, QUARTER, axis=1).transpose(0, 2, 1)
    own, sel, w_out, w_grad = lax.optimization_barrier((own, sel, w_out, w_grad))
    other = lax.ppermute(own, "tile", core)

    partial = pl.pallas_call(
        weight_kernel,
        out_shape=jax.ShapeDtypeStruct((CLASSES, 2, SHARE_ROWS, HALF), f32),
        in_specs=vmem(3),
        out_specs=vmem(1)[0],
        scratch_shapes=[
            *(pltpu.VMEM((n, tiles, HALF), bf16) for n in (CELLS, CELLS, PAD * PAD)),
            pltpu.VMEM((taps * HALF, HALF), f32),
        ],
        compiler_params=PARAMS,
        name="weight_taps",
    )(own, other, sel)

    rows = 2 * SHARE

    def at(slide, x, o, y, i):
        return slide * tiles + device_of(x * 4 + y, i, o)

    groups = [
        [at(s + parity, x, o, y + low, i) for x in range(4) for low in range(2) for parity in range(2)]
        for s in range(0, slides, 2)
        for o in range(2)
        for y in range(0, 4, 2)
        for i in range(2)
    ]
    parts = lax.all_to_all(partial, ("dp", "tile"), 0, 0, tiled=True, axis_index_groups=groups)
    outgoing = jax.ShapeDtypeStruct((chips, CELLS, 2 * QUARTER), bf16)
    back_own, back_other = pl.pallas_call(
        conv_kernel,
        out_shape=[outgoing, outgoing],
        in_specs=vmem(5),
        out_specs=vmem(2),
        scratch_shapes=[pltpu.VMEM((n, tiles, width), bf16) for n in (CELLS, CELLS, PAD * PAD)],
        compiler_params=PARAMS,
        name="conv_taps",
    )(own, other, sel, w_out, w_grad)
    back_other = lax.ppermute(back_other, "tile", core)
    parts, back_own, back_other = lax.optimization_barrier((parts, back_own, back_other))

    part = jnp.sum(parts, axis=0)
    groups = [
        [at(s, x, o, y + low, i) for y in range(0, 4, 2) for s in range(slides)]
        for x in range(4)
        for o in range(2)
        for low in range(2)
        for i in range(2)
    ]
    shares = jnp.broadcast_to(part[:, None], (2, slides, SHARE_ROWS, HALF)).reshape(-1, SHARE_ROWS, HALF)
    parts = lax.all_to_all(shares, ("dp", "tile"), 0, 0, tiled=True, axis_index_groups=groups)
    scale = 1.0 / math.sqrt(slides * tiles * cells)
    packed = pl.pallas_call(
        functools.partial(pack_kernel, scale),
        out_shape=jax.ShapeDtypeStruct((chips, 2 * CELLS + rows, HALF), bf16),
        in_specs=vmem(3),
        out_specs=vmem(1)[0],
        scratch_shapes=[pltpu.VMEM((2 * SHARE_ROWS, HALF), f32)],
        compiler_params=PARAMS,
        name="pack",
    )(back_own, back_other, parts)
    mine = lax.all_to_all(packed, "tile", 0, 0, tiled=True, axis_index_groups=same_core)
    other = lax.ppermute(mine, "tile", core)
    grad_weight = pl.pallas_call(
        rows_kernel,
        out_shape=jax.ShapeDtypeStruct((taps, width, width), bf16),
        in_specs=vmem(2),
        out_specs=vmem(1)[0],
        compiler_params=PARAMS,
        name="rows",
    )(mine, other).reshape(weight.shape)

    out, grad = pl.pallas_call(
        join_kernel,
        out_shape=[jax.ShapeDtypeStruct((cells, width), bf16)] * 2,
        in_specs=[smem, *vmem(2)],
        out_specs=vmem(2),
        compiler_params=PARAMS,
        name="join",
    )(tile_counts, mine, tile_owner)
    return out.reshape(features.shape), grad.reshape(features.shape), grad_weight


def solution(mesh):
    return jax.shard_map(
        local,
        mesh=mesh,
        in_specs=(
            P("dp", "tile", None, None, None),
            P("dp", "tile", None, None, None),
            P(),
            P("dp", None),
            P("dp", None, None),
            P("dp"),
        ),
        out_specs=(P("dp", "tile", None, None, None), P("dp", "tile", None, None, None), P()),
        check_vma=False,
    )
```

```python
import functools
import math

import jax
import jax.numpy as jnp
from jax import lax
from jax.experimental import pallas as pl
from jax.experimental.pallas import tpu as pltpu
from jax.sharding import PartitionSpec as P

SPAN = 4
CELLS = SPAN * SPAN
CLASSES = SPAN * SPAN
PAD = SPAN + 2
HALF = 128
QUARTER = 64
SHARE = 36
LOW = 4
bf16, f32 = jnp.bfloat16, jnp.float32


def device_of(m, hi, ho):
    return m // 4 * 16 + ho * 8 + m % 4 * 2 + hi


def vmem(n):
    return [pl.BlockSpec(memory_space=pltpu.VMEM)] * n


PARAMS = pltpu.CompilerParams(vmem_limit_bytes=24 * 1024 * 1024)


def live_mask(owner, count):
    device = lax.axis_index("tile")
    positions = lax.broadcasted_iota(jnp.int32, owner.shape, 1)
    held = jnp.sum(jnp.where(owner == device, positions, 0).astype(f32), axis=1, keepdims=True)
    return held < count.astype(f32)


def class_order(transposed):
    n = CLASSES * CELLS
    o = lax.broadcasted_iota(jnp.int32, (n, n), 1 if transposed else 0)
    c = lax.broadcasted_iota(jnp.int32, (n, n), 0 if transposed else 1)
    mr, mc, r, k = o >> 6, (o >> 4) & 3, (o >> 2) & 3, o & 3
    return c == (r * SPAN + mr) * 16 + k * SPAN + mc


def swap16():
    o = lax.broadcasted_iota(jnp.int32, (256, 256), 0)
    c = lax.broadcasted_iota(jnp.int32, (256, 256), 1)
    return jnp.where(c == ((o & 15) << 4) + (o >> 4), 1.0, 0.0).astype(bf16)


def dot(a, b):
    return jnp.dot(a, b, preferred_element_type=f32)


def split_kernel(count_ref, owner_hbm, x_hbm, g_hbm, send_ref, owner_ref, x_ref, g_ref, sems):
    pairs = [(owner_hbm, owner_ref), (x_hbm, x_ref), (g_hbm, g_ref)]
    copies = [pltpu.make_async_copy(src, dst, sems.at[n]) for n, (src, dst) in enumerate(pairs)]
    for copy in copies:
        copy.start()
    order = class_order(False)
    for copy in copies:
        copy.wait()
    live = live_mask(owner_ref[...], count_ref[0])
    order = jnp.where(order & live, 1.0, 0.0).astype(bf16)
    x = dot(order, x_ref[...]).astype(bf16)
    g = dot(order, g_ref[...]).astype(bf16)
    for m in range(CLASSES):
        rows = slice(m * CELLS, (m + 1) * CELLS)
        for ho in range(2):
            chip = device_of(m, 0, ho) // 2
            send_ref[chip, :, : 2 * HALF] = x[rows]
            send_ref[chip, :, 2 * HALF :] = g[rows]


def surround(padded, cells, sel_ref):
    def put(d, sources, targets):
        width = cells[0].shape[1]
        got = dot(sel_ref[d], jnp.concatenate([cells[s] for s in sources], axis=1)).astype(bf16)
        for n, (r, c) in enumerate(targets):
            padded[r * PAD + c] = got[:, n * width : (n + 1) * width]

    for r in range(SPAN):
        for c in range(SPAN):
            padded[(r + 1) * PAD + c + 1] = cells[r * SPAN + c]
    last, side = SPAN - 1, range(SPAN)
    put(0, [last * SPAN + last], [(0, 0)])
    put(1, [last * SPAN + c for c in side], [(0, c + 1) for c in side])
    put(2, [last * SPAN], [(0, PAD - 1)])
    put(3, [r * SPAN + last for r in side], [(r + 1, 0) for r in side])
    put(4, [r * SPAN for r in side], [(r + 1, PAD - 1) for r in side])
    put(5, [last], [(PAD - 1, 0)])
    put(6, [c for c in side], [(PAD - 1, c + 1) for c in side])
    put(7, [0], [(PAD - 1, PAD - 1)])


def window(padded, a, b):
    rows = [padded[(r + a) * PAD + c + b] for r in range(SPAN) for c in range(SPAN)]
    return jnp.concatenate(rows, axis=0)


def by_cell(refs, put, lanes):
    swap = swap16()
    chips = refs[0].shape[0]
    for n, ref in enumerate(refs):
        for k in range(0, chips, 16):
            turned = dot(swap, lanes(ref, k).reshape(256, -1)).astype(bf16)
            for s in range(CELLS):
                put(s, slice(n * chips + k, n * chips + k + 16), turned[s * 16 : (s + 1) * 16])


def share_of(m, parity):
    return m // 4 * 4 + m % 2 * 2 + parity, m // 2 % 2


def weight_kernel(own_ref, other_ref, sel_ref, out_ref, x_ref, g_ref, padded, sum_ref):
    device = lax.axis_index("tile")
    low_x, low_g = device % 2 == 0, device // 8 % 2 == 0

    def halves(ref, k):
        rows = ref[k : k + 16]
        x = jnp.where(low_x, rows[:, :, :HALF], rows[:, :, HALF : 2 * HALF])
        g = jnp.where(low_g, rows[:, :, 2 * HALF : 3 * HALF], rows[:, :, 3 * HALF :])
        return jnp.concatenate([x, g], axis=2)

    def put(s, tiles, value):
        x_ref[s, tiles, :] = value[:, :HALF]
        g_ref[s, tiles, :] = value[:, HALF:]

    by_cell((own_ref, other_ref), put, halves)
    surround(padded, [x_ref[s] for s in range(CELLS)], sel_ref)
    grad = g_ref[...].reshape(-1, HALF).T
    taps = [(a, b) for a in range(3) for b in range(3)]
    for n in range(0, len(taps), 2):
        views = [window(padded, a, b) for a, b in taps[n : n + 2]]
        sums = dot(grad, jnp.concatenate(views, axis=1))
        for k in range(len(views)):
            sum_ref[(n + k) * HALF : (n + k + 1) * HALF, :] = sums[:, k * HALF : (k + 1) * HALF].T
    for m in range(CLASSES):
        for parity in range(2):
            piece, half = share_of(m, parity)
            for k in range(SHARE // LOW):
                begin = (m * 2 + parity) * SHARE + k * LOW
                out_ref[piece, half, :, k * HALF : (k + 1) * HALF] = sum_ref[begin : begin + LOW, :]


def conv_kernel(
    own_in_ref, other_in_ref, sel_ref, wo_ref, wg_ref, own_ref, other_ref, x_ref, g_ref, padded
):
    tiles = x_ref.shape[1]
    width = x_ref.shape[2]

    def put(s, where, value):
        x_ref[s, where, :] = value[:, :width]
        g_ref[s, where, :] = value[:, width:]

    by_cell((own_in_ref, other_in_ref), put, lambda ref, k: ref[k : k + 16])

    def taps(cells_ref, w_ref, flip):
        surround(padded, [cells_ref[s] for s in range(CELLS)], sel_ref)
        total = jnp.zeros((CELLS * tiles, QUARTER), f32)
        for a in range(3):
            for b in range(3):
                view = window(padded, 2 - a, 2 - b) if flip else window(padded, a, b)
                total = total + dot(view, w_ref[a * 3 + b])
        return total

    forward = taps(x_ref, wo_ref, False)
    backward = taps(g_ref, wg_ref, True)
    both = jnp.concatenate([forward, backward], axis=1).astype(bf16)
    swap = swap16()
    chips = tiles // 2
    for n, ref in enumerate((own_ref, other_ref)):
        for k in range(0, chips, 16):
            begin = n * chips + k
            rows = [both[s * tiles + begin : s * tiles + begin + 16] for s in range(CELLS)]
            turned = dot(swap, jnp.concatenate(rows, axis=0)).astype(bf16)
            ref[k : k + 16] = turned.reshape(16, CELLS, 2 * QUARTER)


def pack_kernel(scale, own_ref, other_ref, parts_ref, out_ref, piece_ref):
    for parity in range(2):
        total = parts_ref[parity]
        for s in range(parity + 2, parts_ref.shape[0], 2):
            total = total + parts_ref[s]
        for k in range(SHARE // LOW):
            begin = parity * SHARE + k * LOW
            piece_ref[begin : begin + LOW, :] = total[:, k * HALF : (k + 1) * HALF]
    piece = (piece_ref[...] * scale).astype(bf16)
    for chip in range(out_ref.shape[0]):
        out_ref[chip, :CELLS, :] = own_ref[chip]
        out_ref[chip, CELLS : 2 * CELLS, :] = other_ref[chip]
        out_ref[chip, 2 * CELLS :, :] = piece


def join_kernel(count_ref, recv_ref, owner_ref, out_ref, grad_ref):
    live = live_mask(owner_ref[...], count_ref[0])
    order = jnp.where(class_order(True) & live, 1.0, 0.0).astype(bf16)

    core = lax.axis_index("tile") % 2
    classes = []
    for m in range(CLASSES):
        quarters = []
        for hi in range(2):
            for ho in range(2):
                chip = device_of(m, 0, ho) // 2
                begin = pl.multiple_of((hi ^ core) * CELLS, CELLS)
                quarters.append(recv_ref[chip, pl.ds(begin, CELLS), :])
        classes.append(quarters)

    def join(low):
        rows = [jnp.concatenate([part[:, low : low + QUARTER] for part in parts], axis=1) for parts in classes]
        return dot(order, jnp.concatenate(rows, axis=0)).astype(bf16)

    out_ref[...] = join(0)
    grad_ref[...] = join(QUARTER)


def rows_kernel(mine_ref, other_ref, out_ref):
    low = lax.axis_index("tile") % 2 == 0
    taps = out_ref.shape[0]

    def half(ref, ho):
        chips = [device_of(m, 0, ho) // 2 for m in range(CLASSES)]
        return jnp.concatenate([ref[c, 2 * CELLS :, :].astype(f32) for c in chips], axis=0)

    for ho in range(2):
        mine, other = half(mine_ref, ho), half(other_ref, ho)
        columns = slice(ho * HALF, (ho + 1) * HALF)
        for tap in range(taps):
            rows = slice(tap * HALF, (tap + 1) * HALF)
            out_ref[tap, :HALF, columns] = jnp.where(low, mine[rows], other[rows]).astype(bf16)
            out_ref[tap, HALF:, columns] = jnp.where(low, other[rows], mine[rows]).astype(bf16)


def neighbour_table(owner, neighbors, names):
    positions = jnp.arange(owner.shape[0], dtype=jnp.int32)
    beside = jnp.sum(jnp.where(neighbors[:, :, None] == positions, owner + 1, 0), axis=2) - 1
    peer = jnp.sum(jnp.where((owner == names[:, None])[:, :, None], beside[None], 0), axis=1)
    return (peer.T[:, :, None] == names).astype(bf16)


def local(features, cotangent, weight, tile_owner, tile_neighbors, tile_counts):
    tiles = lax.axis_size("tile")
    slides = lax.axis_size("dp")
    device = lax.axis_index("tile")
    hi, ho = device % 2, device // 8 % 2
    width = features.shape[-1]
    cells = features.shape[2] * features.shape[3]
    smem = pl.BlockSpec(memory_space=pltpu.SMEM)
    hbm = pl.BlockSpec(memory_space=pltpu.HBM)

    chips = tiles // 2
    core = [(j, j ^ 1) for j in range(tiles)]
    same_core = [[2 * c + i for c in range(chips)] for i in range(2)]
    send = pl.pallas_call(
        split_kernel,
        out_shape=jax.ShapeDtypeStruct((chips, CELLS, 4 * HALF), bf16),
        in_specs=[smem, hbm, hbm, hbm],
        out_specs=vmem(1)[0],
        scratch_shapes=[
            pltpu.VMEM((1, tiles), jnp.int32),
            pltpu.VMEM((cells, width), bf16),
            pltpu.VMEM((cells, width), bf16),
            pltpu.SemaphoreType.DMA((3,)),
        ],
        name="split",
    )(tile_counts, tile_owner, features.reshape(cells, width), cotangent.reshape(cells, width))
    own = lax.all_to_all(send, "tile", 0, 0, tiled=True, axis_index_groups=same_core)

    side = jnp.arange(chips, dtype=jnp.int32) * 2
    names = jnp.concatenate([side + hi, side + 1 - hi])
    sel = neighbour_table(tile_owner[0], tile_neighbors[0], names)
    taps = weight.shape[0] * weight.shape[1]
    quarter = (2 * hi + ho) * QUARTER
    flat = weight.reshape(taps, width, width)
    w_out = lax.dynamic_slice_in_dim(flat, quarter, QUARTER, axis=2)
    w_grad = lax.dynamic_slice_in_dim(flat, quarter, QUARTER, axis=1).transpose(0, 2, 1)
    own, sel, w_out, w_grad = lax.optimization_barrier((own, sel, w_out, w_grad))
    other = lax.ppermute(own, "tile", core)

    partial = pl.pallas_call(
        weight_kernel,
        out_shape=jax.ShapeDtypeStruct((CLASSES, 2, LOW, SHARE // LOW * HALF), f32),
        in_specs=vmem(3),
        out_specs=vmem(1)[0],
        scratch_shapes=[
            *(pltpu.VMEM((n, tiles, HALF), bf16) for n in (CELLS, CELLS, PAD * PAD)),
            pltpu.VMEM((taps * HALF, HALF), f32),
        ],
        compiler_params=PARAMS,
        name="weight_taps",
    )(own, other, sel)

    rows = 2 * SHARE

    def at(slide, x, o, y, i):
        return slide * tiles + device_of(x * 4 + y, i, o)

    groups = [
        [at(s + parity, x, o, y + low, i) for x in range(4) for low in range(2) for parity in range(2)]
        for s in range(0, slides, 2)
        for o in range(2)
        for y in range(0, 4, 2)
        for i in range(2)
    ]
    parts = lax.all_to_all(partial, ("dp", "tile"), 0, 0, tiled=True, axis_index_groups=groups)
    outgoing = jax.ShapeDtypeStruct((chips, CELLS, 2 * QUARTER), bf16)
    back_own, back_other = pl.pallas_call(
        conv_kernel,
        out_shape=[outgoing, outgoing],
        in_specs=vmem(5),
        out_specs=vmem(2),
        scratch_shapes=[pltpu.VMEM((n, tiles, width), bf16) for n in (CELLS, CELLS, PAD * PAD)],
        compiler_params=PARAMS,
        name="conv_taps",
    )(own, other, sel, w_out, w_grad)
    back_other = lax.ppermute(back_other, "tile", core)
    parts, back_own, back_other = lax.optimization_barrier((parts, back_own, back_other))

    part = jnp.sum(parts, axis=0)
    groups = [
        [at(s, x, o, y + low, i) for y in range(0, 4, 2) for s in range(slides)]
        for x in range(4)
        for o in range(2)
        for low in range(2)
        for i in range(2)
    ]
    shares = jnp.broadcast_to(part[:, None], (2, slides, *part.shape[1:])).reshape(-1, *part.shape[1:])
    parts = lax.all_to_all(shares, ("dp", "tile"), 0, 0, tiled=True, axis_index_groups=groups)
    scale = 1.0 / math.sqrt(slides * tiles * cells)
    packed = pl.pallas_call(
        functools.partial(pack_kernel, scale),
        out_shape=jax.ShapeDtypeStruct((chips, 2 * CELLS + rows, HALF), bf16),
        in_specs=vmem(3),
        out_specs=vmem(1)[0],
        scratch_shapes=[pltpu.VMEM((2 * SHARE, HALF), f32)],
        compiler_params=PARAMS,
        name="pack",
    )(back_own, back_other, parts)
    mine = lax.all_to_all(packed, "tile", 0, 0, tiled=True, axis_index_groups=same_core)
    other = lax.ppermute(mine, "tile", core)
    grad_weight = pl.pallas_call(
        rows_kernel,
        out_shape=jax.ShapeDtypeStruct((taps, width, width), bf16),
        in_specs=vmem(2),
        out_specs=vmem(1)[0],
        compiler_params=PARAMS,
        name="rows",
    )(mine, other).reshape(weight.shape)

    out, grad = pl.pallas_call(
        join_kernel,
        out_shape=[jax.ShapeDtypeStruct((cells, width), bf16)] * 2,
        in_specs=[smem, *vmem(2)],
        out_specs=vmem(2),
        compiler_params=PARAMS,
        name="join",
    )(tile_counts, mine, tile_owner)
    return out.reshape(features.shape), grad.reshape(features.shape), grad_weight


def solution(mesh):
    return jax.shard_map(
        local,
        mesh=mesh,
        in_specs=(
            P("dp", "tile", None, None, None),
            P("dp", "tile", None, None, None),
            P(),
            P("dp", None),
            P("dp", None, None),
            P("dp"),
        ),
        out_specs=(P("dp", "tile", None, None, None), P("dp", "tile", None, None, None), P()),
        check_vma=False,
    )
```

```python
import functools
import math

import jax
import jax.numpy as jnp
from jax import lax
from jax.experimental import pallas as pl
from jax.experimental.pallas import tpu as pltpu
from jax.sharding import PartitionSpec as P

SPAN = 4
CELLS = SPAN * SPAN
CLASSES = SPAN * SPAN
PAD = SPAN + 2
HALF = 128
QUARTER = 64
SHARE = 36
LOW = 4
bf16, f32 = jnp.bfloat16, jnp.float32


def device_of(m, hi, ho):
    return m // 4 * 16 + ho * 8 + m % 4 * 2 + hi


def vmem(n):
    return [pl.BlockSpec(memory_space=pltpu.VMEM)] * n


PARAMS = pltpu.CompilerParams(vmem_limit_bytes=24 * 1024 * 1024)


def live_mask(owner, count):
    device = lax.axis_index("tile")
    positions = lax.broadcasted_iota(jnp.int32, owner.shape, 1)
    held = jnp.sum(jnp.where(owner == device, positions, 0).astype(f32), axis=1, keepdims=True)
    return held < count.astype(f32)


def class_order(transposed):
    n = CLASSES * CELLS
    o = lax.broadcasted_iota(jnp.int32, (n, n), 1 if transposed else 0)
    c = lax.broadcasted_iota(jnp.int32, (n, n), 0 if transposed else 1)
    mr, mc, r, k = o >> 6, (o >> 4) & 3, (o >> 2) & 3, o & 3
    return c == (r * SPAN + mr) * 16 + k * SPAN + mc


def swap16():
    o = lax.broadcasted_iota(jnp.int32, (256, 256), 0)
    c = lax.broadcasted_iota(jnp.int32, (256, 256), 1)
    return jnp.where(c == ((o & 15) << 4) + (o >> 4), 1.0, 0.0).astype(bf16)


def dot(a, b):
    return jnp.dot(a, b, preferred_element_type=f32)


def split_kernel(count_ref, owner_hbm, x_hbm, g_hbm, send_ref, owner_ref, x_ref, g_ref, sems):
    pairs = [(owner_hbm, owner_ref), (x_hbm, x_ref), (g_hbm, g_ref)]
    copies = [pltpu.make_async_copy(src, dst, sems.at[n]) for n, (src, dst) in enumerate(pairs)]
    for copy in copies:
        copy.start()
    order = class_order(False)
    for copy in copies:
        copy.wait()
    live = live_mask(owner_ref[...], count_ref[0])
    order = jnp.where(order & live, 1.0, 0.0).astype(bf16)
    x = dot(order, x_ref[...]).astype(bf16)
    g = dot(order, g_ref[...]).astype(bf16)
    for m in range(CLASSES):
        rows = slice(m * CELLS, (m + 1) * CELLS)
        for ho in range(2):
            chip = device_of(m, 0, ho) // 2
            send_ref[chip, :, : 2 * HALF] = x[rows]
            send_ref[chip, :, 2 * HALF :] = g[rows]


def surround(padded, cells, sel_ref):
    def put(d, sources, targets):
        width = cells[0].shape[1]
        got = dot(sel_ref[d], jnp.concatenate([cells[s] for s in sources], axis=1)).astype(bf16)
        for n, (r, c) in enumerate(targets):
            padded[r * PAD + c] = got[:, n * width : (n + 1) * width]

    for r in range(SPAN):
        for c in range(SPAN):
            padded[(r + 1) * PAD + c + 1] = cells[r * SPAN + c]
    last, side = SPAN - 1, range(SPAN)
    put(0, [last * SPAN + last], [(0, 0)])
    put(1, [last * SPAN + c for c in side], [(0, c + 1) for c in side])
    put(2, [last * SPAN], [(0, PAD - 1)])
    put(3, [r * SPAN + last for r in side], [(r + 1, 0) for r in side])
    put(4, [r * SPAN for r in side], [(r + 1, PAD - 1) for r in side])
    put(5, [last], [(PAD - 1, 0)])
    put(6, [c for c in side], [(PAD - 1, c + 1) for c in side])
    put(7, [0], [(PAD - 1, PAD - 1)])


def window(padded, a, b):
    rows = [padded[(r + a) * PAD + c + b] for r in range(SPAN) for c in range(SPAN)]
    return jnp.concatenate(rows, axis=0)


def by_cell(refs, put, lanes):
    swap = swap16()
    chips = refs[0].shape[0]
    for n, ref in enumerate(refs):
        for k in range(0, chips, 16):
            turned = dot(swap, lanes(ref, k).reshape(256, -1)).astype(bf16)
            for s in range(CELLS):
                put(s, slice(n * chips + k, n * chips + k + 16), turned[s * 16 : (s + 1) * 16])


def share_of(m, parity):
    return m // 4 * 4 + m % 2 * 2 + parity, m // 2 % 2


def weight_kernel(own_ref, other_ref, sel_ref, out_ref, x_ref, g_ref, padded, sum_ref):
    device = lax.axis_index("tile")
    low_x, low_g = device % 2 == 0, device // 8 % 2 == 0

    def halves(ref, k):
        rows = ref[k : k + 16]
        x = jnp.where(low_x, rows[:, :, :HALF], rows[:, :, HALF : 2 * HALF])
        g = jnp.where(low_g, rows[:, :, 2 * HALF : 3 * HALF], rows[:, :, 3 * HALF :])
        return jnp.concatenate([x, g], axis=2)

    def put(s, tiles, value):
        x_ref[s, tiles, :] = value[:, :HALF]
        g_ref[s, tiles, :] = value[:, HALF:]

    by_cell((own_ref, other_ref), put, halves)
    surround(padded, [x_ref[s] for s in range(CELLS)], sel_ref)
    grad = g_ref[...].reshape(-1, HALF).T
    taps = [(a, b) for a in range(3) for b in range(3)]
    for n in range(0, len(taps), 2):
        views = [window(padded, a, b) for a, b in taps[n : n + 2]]
        sums = dot(grad, jnp.concatenate(views, axis=1))
        for k in range(len(views)):
            sum_ref[(n + k) * HALF : (n + k + 1) * HALF, :] = sums[:, k * HALF : (k + 1) * HALF].T
    for m in range(CLASSES):
        for parity in range(2):
            piece, half = share_of(m, parity)
            for k in range(SHARE // LOW):
                begin = (m * 2 + parity) * SHARE + k * LOW
                out_ref[piece, half, :, k * HALF : (k + 1) * HALF] = sum_ref[begin : begin + LOW, :]


def conv_kernel(
    own_in_ref, other_in_ref, sel_ref, wo_ref, wg_ref, own_ref, other_ref, x_ref, g_ref, padded
):
    tiles = x_ref.shape[1]
    width = x_ref.shape[2]

    def put(s, where, value):
        x_ref[s, where, :] = value[:, :width]
        g_ref[s, where, :] = value[:, width:]

    by_cell((own_in_ref, other_in_ref), put, lambda ref, k: ref[k : k + 16])

    def taps(cells_ref, w_ref, flip):
        surround(padded, [cells_ref[s] for s in range(CELLS)], sel_ref)
        total = jnp.zeros((CELLS * tiles, QUARTER), f32)
        for a in range(3):
            for b in range(3):
                view = window(padded, 2 - a, 2 - b) if flip else window(padded, a, b)
                total = total + dot(view, w_ref[a * 3 + b])
        return total

    forward = taps(x_ref, wo_ref, False)
    backward = taps(g_ref, wg_ref, True)
    both = jnp.concatenate([forward, backward], axis=1).astype(bf16)
    swap = swap16()
    chips = tiles // 2
    for n, ref in enumerate((own_ref, other_ref)):
        for k in range(0, chips, 16):
            begin = n * chips + k
            rows = [both[s * tiles + begin : s * tiles + begin + 16] for s in range(CELLS)]
            turned = dot(swap, jnp.concatenate(rows, axis=0)).astype(bf16)
            ref[k : k + 16] = turned.reshape(16, CELLS, 2 * QUARTER)


def pack_kernel(scale, own_ref, other_ref, parts_ref, out_ref, piece_ref):
    for parity in range(2):
        total = parts_ref[parity]
        for s in range(parity + 2, parts_ref.shape[0], 2):
            total = total + parts_ref[s]
        for k in range(SHARE // LOW):
            begin = parity * SHARE + k * LOW
            piece_ref[begin : begin + LOW, :] = total[:, k * HALF : (k + 1) * HALF]
    piece = (piece_ref[...] * scale).astype(bf16)
    for chip in range(out_ref.shape[0]):
        out_ref[chip, :CELLS, :] = own_ref[chip]
        out_ref[chip, CELLS : 2 * CELLS, :] = other_ref[chip]
        out_ref[chip, 2 * CELLS :, :] = piece


def join_kernel(count_ref, recv_ref, owner_ref, out_ref, grad_ref):
    live = live_mask(owner_ref[...], count_ref[0])
    order = jnp.where(class_order(True) & live, 1.0, 0.0).astype(bf16)

    core = lax.axis_index("tile") % 2
    classes = []
    for m in range(CLASSES):
        quarters = []
        for hi in range(2):
            for ho in range(2):
                chip = device_of(m, 0, ho) // 2
                begin = pl.multiple_of((hi ^ core) * CELLS, CELLS)
                quarters.append(recv_ref[chip, pl.ds(begin, CELLS), :])
        classes.append(quarters)

    def join(low):
        rows = [jnp.concatenate([part[:, low : low + QUARTER] for part in parts], axis=1) for parts in classes]
        return dot(order, jnp.concatenate(rows, axis=0)).astype(bf16)

    out_ref[...] = join(0)
    grad_ref[...] = join(QUARTER)


def rows_kernel(mine_ref, other_ref, out_hbm, out_ref, sems):
    low = lax.axis_index("tile") % 2 == 0
    taps = out_ref.shape[0]

    def half(ref, ho):
        chips = [device_of(m, 0, ho) // 2 for m in range(CLASSES)]
        return jnp.concatenate([ref[c].astype(f32) for c in chips], axis=0)

    halves = [(half(mine_ref, ho), half(other_ref, ho)) for ho in range(2)]
    copies = []
    for tap in range(taps):
        rows = slice(tap * HALF, (tap + 1) * HALF)
        for ho, (mine, other) in enumerate(halves):
            columns = slice(ho * HALF, (ho + 1) * HALF)
            out_ref[tap, :HALF, columns] = jnp.where(low, mine[rows], other[rows]).astype(bf16)
            out_ref[tap, HALF:, columns] = jnp.where(low, other[rows], mine[rows]).astype(bf16)
        copies.append(pltpu.make_async_copy(out_ref.at[tap], out_hbm.at[tap], sems.at[tap]))
        copies[-1].start()
    for copy in copies:
        copy.wait()


def neighbour_table(owner, neighbors, names):
    positions = jnp.arange(owner.shape[0], dtype=jnp.int32)
    beside = jnp.sum(jnp.where(neighbors[:, :, None] == positions, owner + 1, 0), axis=2) - 1
    peer = jnp.sum(jnp.where((owner == names[:, None])[:, :, None], beside[None], 0), axis=1)
    return (peer.T[:, :, None] == names).astype(bf16)


def local(features, cotangent, weight, tile_owner, tile_neighbors, tile_counts):
    tiles = lax.axis_size("tile")
    slides = lax.axis_size("dp")
    device = lax.axis_index("tile")
    hi, ho = device % 2, device // 8 % 2
    width = features.shape[-1]
    cells = features.shape[2] * features.shape[3]
    smem = pl.BlockSpec(memory_space=pltpu.SMEM)
    hbm = pl.BlockSpec(memory_space=pltpu.HBM)

    chips = tiles // 2
    core = [(j, j ^ 1) for j in range(tiles)]
    same_core = [[2 * c + i for c in range(chips)] for i in range(2)]
    send = pl.pallas_call(
        split_kernel,
        out_shape=jax.ShapeDtypeStruct((chips, CELLS, 4 * HALF), bf16),
        in_specs=[smem, hbm, hbm, hbm],
        out_specs=vmem(1)[0],
        scratch_shapes=[
            pltpu.VMEM((1, tiles), jnp.int32),
            pltpu.VMEM((cells, width), bf16),
            pltpu.VMEM((cells, width), bf16),
            pltpu.SemaphoreType.DMA((3,)),
        ],
        name="split",
    )(tile_counts, tile_owner, features.reshape(cells, width), cotangent.reshape(cells, width))
    own = lax.all_to_all(send, "tile", 0, 0, tiled=True, axis_index_groups=same_core)

    side = jnp.arange(chips, dtype=jnp.int32) * 2
    names = jnp.concatenate([side + hi, side + 1 - hi])
    sel = neighbour_table(tile_owner[0], tile_neighbors[0], names)
    taps = weight.shape[0] * weight.shape[1]
    quarter = (2 * hi + ho) * QUARTER
    flat = weight.reshape(taps, width, width)
    w_out = lax.dynamic_slice_in_dim(flat, quarter, QUARTER, axis=2)
    w_grad = lax.dynamic_slice_in_dim(flat, quarter, QUARTER, axis=1).transpose(0, 2, 1)
    own, sel, w_out, w_grad = lax.optimization_barrier((own, sel, w_out, w_grad))
    other = lax.ppermute(own, "tile", core)

    partial = pl.pallas_call(
        weight_kernel,
        out_shape=jax.ShapeDtypeStruct((CLASSES, 2, LOW, SHARE // LOW * HALF), f32),
        in_specs=vmem(3),
        out_specs=vmem(1)[0],
        scratch_shapes=[
            *(pltpu.VMEM((n, tiles, HALF), bf16) for n in (CELLS, CELLS, PAD * PAD)),
            pltpu.VMEM((taps * HALF, HALF), f32),
        ],
        compiler_params=PARAMS,
        name="weight_taps",
    )(own, other, sel)

    rows = 2 * SHARE

    def at(slide, x, o, y, i):
        return slide * tiles + device_of(x * 4 + y, i, o)

    groups = [
        [at(s + parity, x, o, y + low, i) for x in range(4) for low in range(2) for parity in range(2)]
        for s in range(0, slides, 2)
        for o in range(2)
        for y in range(0, 4, 2)
        for i in range(2)
    ]
    parts = lax.all_to_all(partial, ("dp", "tile"), 0, 0, tiled=True, axis_index_groups=groups)
    outgoing = jax.ShapeDtypeStruct((chips, CELLS, 2 * QUARTER), bf16)
    back_own, back_other = pl.pallas_call(
        conv_kernel,
        out_shape=[outgoing, outgoing],
        in_specs=vmem(5),
        out_specs=vmem(2),
        scratch_shapes=[pltpu.VMEM((n, tiles, width), bf16) for n in (CELLS, CELLS, PAD * PAD)],
        compiler_params=PARAMS,
        name="conv_taps",
    )(own, other, sel, w_out, w_grad)
    back_other = lax.ppermute(back_other, "tile", core)
    parts, back_own, back_other = lax.optimization_barrier((parts, back_own, back_other))

    part = jnp.sum(parts, axis=0)
    groups = [
        [at(s, x, o, y + low, i) for y in range(0, 4, 2) for s in range(slides)]
        for x in range(4)
        for o in range(2)
        for low in range(2)
        for i in range(2)
    ]
    shares = jnp.broadcast_to(part[:, None], (2, slides, *part.shape[1:])).reshape(-1, *part.shape[1:])
    parts = lax.all_to_all(shares, ("dp", "tile"), 0, 0, tiled=True, axis_index_groups=groups)
    scale = 1.0 / math.sqrt(slides * tiles * cells)
    packed = pl.pallas_call(
        functools.partial(pack_kernel, scale),
        out_shape=jax.ShapeDtypeStruct((chips, 2 * CELLS + rows, HALF), bf16),
        in_specs=vmem(3),
        out_specs=vmem(1)[0],
        scratch_shapes=[pltpu.VMEM((2 * SHARE, HALF), f32)],
        compiler_params=PARAMS,
        name="pack",
    )(back_own, back_other, parts)
    mine = lax.all_to_all(packed, "tile", 0, 0, tiled=True, axis_index_groups=same_core)
    pieces = mine[:, 2 * CELLS :, :]
    other = lax.ppermute(pieces, "tile", core)
    grad_weight = pl.pallas_call(
        rows_kernel,
        out_shape=jax.ShapeDtypeStruct((taps, width, width), bf16),
        in_specs=vmem(2),
        out_specs=hbm,
        scratch_shapes=[pltpu.VMEM((taps, width, width), bf16), pltpu.SemaphoreType.DMA((taps,))],
        compiler_params=PARAMS,
        name="rows",
    )(pieces, other).reshape(weight.shape)

    out, grad = pl.pallas_call(
        join_kernel,
        out_shape=[jax.ShapeDtypeStruct((cells, width), bf16)] * 2,
        in_specs=[smem, *vmem(2)],
        out_specs=vmem(2),
        compiler_params=PARAMS,
        name="join",
    )(tile_counts, mine, tile_owner)
    return out.reshape(features.shape), grad.reshape(features.shape), grad_weight


def solution(mesh):
    return jax.shard_map(
        local,
        mesh=mesh,
        in_specs=(
            P("dp", "tile", None, None, None),
            P("dp", "tile", None, None, None),
            P(),
            P("dp", None),
            P("dp", None, None),
            P("dp"),
        ),
        out_specs=(P("dp", "tile", None, None, None), P("dp", "tile", None, None, None), P()),
        check_vma=False,
    )
```

```python
import functools
import math

import jax
import jax.numpy as jnp
from jax import lax
from jax.experimental import pallas as pl
from jax.experimental.pallas import tpu as pltpu
from jax.sharding import PartitionSpec as P

SPAN = 4
CELLS = SPAN * SPAN
CLASSES = SPAN * SPAN
PAD = SPAN + 2
HALF = 128
QUARTER = 64
SHARE = 36
LOW = 4
bf16, f32 = jnp.bfloat16, jnp.float32


def device_of(m, hi, ho):
    return m // 4 * 16 + ho * 8 + m % 4 * 2 + hi


def vmem(n):
    return [pl.BlockSpec(memory_space=pltpu.VMEM)] * n


PARAMS = pltpu.CompilerParams(vmem_limit_bytes=24 * 1024 * 1024)


def live_mask(owner, count):
    device = lax.axis_index("tile")
    positions = lax.broadcasted_iota(jnp.int32, owner.shape, 1)
    held = jnp.sum(jnp.where(owner == device, positions, 0).astype(f32), axis=1, keepdims=True)
    return held < count.astype(f32)


def class_order(transposed):
    n = CLASSES * CELLS
    o = lax.broadcasted_iota(jnp.int32, (n, n), 1 if transposed else 0)
    c = lax.broadcasted_iota(jnp.int32, (n, n), 0 if transposed else 1)
    mr, mc, r, k = o >> 6, (o >> 4) & 3, (o >> 2) & 3, o & 3
    return c == (r * SPAN + mr) * 16 + k * SPAN + mc


def swap16():
    o = lax.broadcasted_iota(jnp.int32, (256, 256), 0)
    c = lax.broadcasted_iota(jnp.int32, (256, 256), 1)
    return jnp.where(c == ((o & 15) << 4) + (o >> 4), 1.0, 0.0).astype(bf16)


def dot(a, b):
    return jnp.dot(a, b, preferred_element_type=f32)


def split_kernel(count_ref, owner_hbm, x_hbm, g_hbm, send_hbm, send_ref, owner_ref, x_ref, g_ref, sems, out_sems):
    pairs = [(owner_hbm, owner_ref), (x_hbm, x_ref), (g_hbm, g_ref)]
    copies = [pltpu.make_async_copy(src, dst, sems.at[n]) for n, (src, dst) in enumerate(pairs)]
    for copy in copies:
        copy.start()
    order = class_order(False)
    for copy in copies:
        copy.wait()
    live = live_mask(owner_ref[...], count_ref[0])
    order = jnp.where(order & live, 1.0, 0.0).astype(bf16)
    column = send_ref.shape[0] // 4
    outs = []
    for n in range(4):
        block = order[n * 4 * CELLS : (n + 1) * 4 * CELLS]
        x = dot(block, x_ref[...]).astype(bf16)
        g = dot(block, g_ref[...]).astype(bf16)
        for k in range(4):
            rows = slice(k * CELLS, (k + 1) * CELLS)
            for ho in range(2):
                chip = device_of(n * 4 + k, 0, ho) // 2
                send_ref[chip, :, : 2 * HALF] = x[rows]
                send_ref[chip, :, 2 * HALF :] = g[rows]
        part = pl.ds(n * column, column)
        outs.append(pltpu.make_async_copy(send_ref.at[part], send_hbm.at[part], out_sems.at[n]))
        outs[-1].start()
    for copy in outs:
        copy.wait()


def surround(padded, cells, sel_ref):
    def put(d, sources, targets):
        width = cells[0].shape[1]
        got = dot(sel_ref[d], jnp.concatenate([cells[s] for s in sources], axis=1)).astype(bf16)
        for n, (r, c) in enumerate(targets):
            padded[r * PAD + c] = got[:, n * width : (n + 1) * width]

    for r in range(SPAN):
        for c in range(SPAN):
            padded[(r + 1) * PAD + c + 1] = cells[r * SPAN + c]
    last, side = SPAN - 1, range(SPAN)
    put(0, [last * SPAN + last], [(0, 0)])
    put(1, [last * SPAN + c for c in side], [(0, c + 1) for c in side])
    put(2, [last * SPAN], [(0, PAD - 1)])
    put(3, [r * SPAN + last for r in side], [(r + 1, 0) for r in side])
    put(4, [r * SPAN for r in side], [(r + 1, PAD - 1) for r in side])
    put(5, [last], [(PAD - 1, 0)])
    put(6, [c for c in side], [(PAD - 1, c + 1) for c in side])
    put(7, [0], [(PAD - 1, PAD - 1)])


def window(padded, a, b):
    rows = [padded[(r + a) * PAD + c + b] for r in range(SPAN) for c in range(SPAN)]
    return jnp.concatenate(rows, axis=0)


def by_cell(refs, put, lanes):
    swap = swap16()
    chips = refs[0].shape[0]
    for n, ref in enumerate(refs):
        for k in range(0, chips, 16):
            turned = dot(swap, lanes(ref, k).reshape(256, -1)).astype(bf16)
            for s in range(CELLS):
                put(s, slice(n * chips + k, n * chips + k + 16), turned[s * 16 : (s + 1) * 16])


def share_of(m, parity):
    return m // 4 * 4 + m % 2 * 2 + parity, m // 2 % 2


def weight_kernel(own_ref, other_ref, sel_ref, out_ref, x_ref, g_ref, padded, sum_ref):
    device = lax.axis_index("tile")
    low_x, low_g = device % 2 == 0, device // 8 % 2 == 0

    def halves(ref, k):
        rows = ref[k : k + 16]
        x = jnp.where(low_x, rows[:, :, :HALF], rows[:, :, HALF : 2 * HALF])
        g = jnp.where(low_g, rows[:, :, 2 * HALF : 3 * HALF], rows[:, :, 3 * HALF :])
        return jnp.concatenate([x, g], axis=2)

    def put(s, tiles, value):
        x_ref[s, tiles, :] = value[:, :HALF]
        g_ref[s, tiles, :] = value[:, HALF:]

    by_cell((own_ref, other_ref), put, halves)
    surround(padded, [x_ref[s] for s in range(CELLS)], sel_ref)
    grad = g_ref[...].reshape(-1, HALF).T
    taps = [(a, b) for a in range(3) for b in range(3)]
    for n in range(0, len(taps), 2):
        views = [window(padded, a, b) for a, b in taps[n : n + 2]]
        sums = dot(grad, jnp.concatenate(views, axis=1))
        for k in range(len(views)):
            sum_ref[(n + k) * HALF : (n + k + 1) * HALF, :] = sums[:, k * HALF : (k + 1) * HALF].T
    for m in range(CLASSES):
        for parity in range(2):
            piece, half = share_of(m, parity)
            for k in range(SHARE // LOW):
                begin = (m * 2 + parity) * SHARE + k * LOW
                out_ref[piece, half, :, k * HALF : (k + 1) * HALF] = sum_ref[begin : begin + LOW, :]


def conv_kernel(
    own_in_ref, other_in_ref, sel_ref, wo_ref, wg_ref, own_ref, other_ref, x_ref, g_ref, padded
):
    tiles = x_ref.shape[1]
    width = x_ref.shape[2]

    def put(s, where, value):
        x_ref[s, where, :] = value[:, :width]
        g_ref[s, where, :] = value[:, width:]

    by_cell((own_in_ref, other_in_ref), put, lambda ref, k: ref[k : k + 16])

    def taps(cells_ref, w_ref, flip):
        surround(padded, [cells_ref[s] for s in range(CELLS)], sel_ref)
        total = jnp.zeros((CELLS * tiles, QUARTER), f32)
        for a in range(3):
            for b in range(3):
                view = window(padded, 2 - a, 2 - b) if flip else window(padded, a, b)
                total = total + dot(view, w_ref[a * 3 + b])
        return total

    forward = taps(x_ref, wo_ref, False)
    backward = taps(g_ref, wg_ref, True)
    both = jnp.concatenate([forward, backward], axis=1).astype(bf16)
    swap = swap16()
    chips = tiles // 2
    for n, ref in enumerate((own_ref, other_ref)):
        for k in range(0, chips, 16):
            begin = n * chips + k
            rows = [both[s * tiles + begin : s * tiles + begin + 16] for s in range(CELLS)]
            turned = dot(swap, jnp.concatenate(rows, axis=0)).astype(bf16)
            ref[k : k + 16] = turned.reshape(16, CELLS, 2 * QUARTER)


def pack_kernel(scale, own_ref, other_ref, parts_ref, out_ref, piece_ref):
    for parity in range(2):
        total = parts_ref[parity]
        for s in range(parity + 2, parts_ref.shape[0], 2):
            total = total + parts_ref[s]
        for k in range(SHARE // LOW):
            begin = parity * SHARE + k * LOW
            piece_ref[begin : begin + LOW, :] = total[:, k * HALF : (k + 1) * HALF]
    piece = (piece_ref[...] * scale).astype(bf16)
    for chip in range(out_ref.shape[0]):
        out_ref[chip, :CELLS, :] = own_ref[chip]
        out_ref[chip, CELLS : 2 * CELLS, :] = other_ref[chip]
        out_ref[chip, 2 * CELLS :, :] = piece


def join_kernel(count_ref, recv_ref, owner_ref, out_ref, grad_ref):
    live = live_mask(owner_ref[...], count_ref[0])
    order = jnp.where(class_order(True) & live, 1.0, 0.0).astype(bf16)

    core = lax.axis_index("tile") % 2
    classes = []
    for m in range(CLASSES):
        quarters = []
        for hi in range(2):
            for ho in range(2):
                chip = device_of(m, 0, ho) // 2
                begin = pl.multiple_of((hi ^ core) * CELLS, CELLS)
                quarters.append(recv_ref[chip, pl.ds(begin, CELLS), :])
        classes.append(quarters)

    def join(low):
        rows = [jnp.concatenate([part[:, low : low + QUARTER] for part in parts], axis=1) for parts in classes]
        return dot(order, jnp.concatenate(rows, axis=0)).astype(bf16)

    out_ref[...] = join(0)
    grad_ref[...] = join(QUARTER)


def rows_kernel(mine_ref, other_ref, out_hbm, out_ref, sems):
    low = lax.axis_index("tile") % 2 == 0
    taps = out_ref.shape[0]

    def half(ref, ho):
        chips = [device_of(m, 0, ho) // 2 for m in range(CLASSES)]
        return jnp.concatenate([ref[c].astype(f32) for c in chips], axis=0)

    halves = [(half(mine_ref, ho), half(other_ref, ho)) for ho in range(2)]
    copies = []
    for tap in range(taps):
        rows = slice(tap * HALF, (tap + 1) * HALF)
        for ho, (mine, other) in enumerate(halves):
            columns = slice(ho * HALF, (ho + 1) * HALF)
            out_ref[tap, :HALF, columns] = jnp.where(low, mine[rows], other[rows]).astype(bf16)
            out_ref[tap, HALF:, columns] = jnp.where(low, other[rows], mine[rows]).astype(bf16)
        copies.append(pltpu.make_async_copy(out_ref.at[tap], out_hbm.at[tap], sems.at[tap]))
        copies[-1].start()
    for copy in copies:
        copy.wait()


def neighbour_table(owner, neighbors, names):
    positions = jnp.arange(owner.shape[0], dtype=jnp.int32)
    beside = jnp.sum(jnp.where(neighbors[:, :, None] == positions, owner + 1, 0), axis=2) - 1
    peer = jnp.sum(jnp.where((owner == names[:, None])[:, :, None], beside[None], 0), axis=1)
    return (peer.T[:, :, None] == names).astype(bf16)


def local(features, cotangent, weight, tile_owner, tile_neighbors, tile_counts):
    tiles = lax.axis_size("tile")
    slides = lax.axis_size("dp")
    device = lax.axis_index("tile")
    hi, ho = device % 2, device // 8 % 2
    width = features.shape[-1]
    cells = features.shape[2] * features.shape[3]
    smem = pl.BlockSpec(memory_space=pltpu.SMEM)
    hbm = pl.BlockSpec(memory_space=pltpu.HBM)

    chips = tiles // 2
    core = [(j, j ^ 1) for j in range(tiles)]
    same_core = [[2 * c + i for c in range(chips)] for i in range(2)]
    send = pl.pallas_call(
        split_kernel,
        out_shape=jax.ShapeDtypeStruct((chips, CELLS, 4 * HALF), bf16),
        in_specs=[smem, hbm, hbm, hbm],
        out_specs=hbm,
        scratch_shapes=[
            pltpu.VMEM((chips, CELLS, 4 * HALF), bf16),
            pltpu.VMEM((1, tiles), jnp.int32),
            pltpu.VMEM((cells, width), bf16),
            pltpu.VMEM((cells, width), bf16),
            pltpu.SemaphoreType.DMA((3,)),
            pltpu.SemaphoreType.DMA((4,)),
        ],
        name="split",
    )(tile_counts, tile_owner, features.reshape(cells, width), cotangent.reshape(cells, width))
    own = lax.all_to_all(send, "tile", 0, 0, tiled=True, axis_index_groups=same_core)

    side = jnp.arange(chips, dtype=jnp.int32) * 2
    names = jnp.concatenate([side + hi, side + 1 - hi])
    sel = neighbour_table(tile_owner[0], tile_neighbors[0], names)
    taps = weight.shape[0] * weight.shape[1]
    quarter = (2 * hi + ho) * QUARTER
    flat = weight.reshape(taps, width, width)
    w_out = lax.dynamic_slice_in_dim(flat, quarter, QUARTER, axis=2)
    w_grad = lax.dynamic_slice_in_dim(flat, quarter, QUARTER, axis=1).transpose(0, 2, 1)
    own, sel, w_out, w_grad = lax.optimization_barrier((own, sel, w_out, w_grad))
    other = lax.ppermute(own, "tile", core)

    partial = pl.pallas_call(
        weight_kernel,
        out_shape=jax.ShapeDtypeStruct((CLASSES, 2, LOW, SHARE // LOW * HALF), f32),
        in_specs=vmem(3),
        out_specs=vmem(1)[0],
        scratch_shapes=[
            *(pltpu.VMEM((n, tiles, HALF), bf16) for n in (CELLS, CELLS, PAD * PAD)),
            pltpu.VMEM((taps * HALF, HALF), f32),
        ],
        compiler_params=PARAMS,
        name="weight_taps",
    )(own, other, sel)

    rows = 2 * SHARE

    def at(slide, x, o, y, i):
        return slide * tiles + device_of(x * 4 + y, i, o)

    groups = [
        [at(s + parity, x, o, y + low, i) for x in range(4) for low in range(2) for parity in range(2)]
        for s in range(0, slides, 2)
        for o in range(2)
        for y in range(0, 4, 2)
        for i in range(2)
    ]
    parts = lax.all_to_all(partial, ("dp", "tile"), 0, 0, tiled=True, axis_index_groups=groups)
    outgoing = jax.ShapeDtypeStruct((chips, CELLS, 2 * QUARTER), bf16)
    back_own, back_other = pl.pallas_call(
        conv_kernel,
        out_shape=[outgoing, outgoing],
        in_specs=vmem(5),
        out_specs=vmem(2),
        scratch_shapes=[pltpu.VMEM((n, tiles, width), bf16) for n in (CELLS, CELLS, PAD * PAD)],
        compiler_params=PARAMS,
        name="conv_taps",
    )(own, other, sel, w_out, w_grad)
    back_other = lax.ppermute(back_other, "tile", core)
    parts, back_own, back_other = lax.optimization_barrier((parts, back_own, back_other))

    part = jnp.sum(parts, axis=0)
    groups = [
        [at(s, x, o, y + low, i) for y in range(0, 4, 2) for s in range(slides)]
        for x in range(4)
        for o in range(2)
        for low in range(2)
        for i in range(2)
    ]
    shares = jnp.broadcast_to(part[:, None], (2, slides, *part.shape[1:])).reshape(-1, *part.shape[1:])
    parts = lax.all_to_all(shares, ("dp", "tile"), 0, 0, tiled=True, axis_index_groups=groups)
    scale = 1.0 / math.sqrt(slides * tiles * cells)
    packed = pl.pallas_call(
        functools.partial(pack_kernel, scale),
        out_shape=jax.ShapeDtypeStruct((chips, 2 * CELLS + rows, HALF), bf16),
        in_specs=vmem(3),
        out_specs=vmem(1)[0],
        scratch_shapes=[pltpu.VMEM((2 * SHARE, HALF), f32)],
        compiler_params=PARAMS,
        name="pack",
    )(back_own, back_other, parts)
    mine = lax.all_to_all(packed, "tile", 0, 0, tiled=True, axis_index_groups=same_core)
    pieces = mine[:, 2 * CELLS :, :]
    other = lax.ppermute(pieces, "tile", core)
    grad_weight = pl.pallas_call(
        rows_kernel,
        out_shape=jax.ShapeDtypeStruct((taps, width, width), bf16),
        in_specs=vmem(2),
        out_specs=hbm,
        scratch_shapes=[pltpu.VMEM((taps, width, width), bf16), pltpu.SemaphoreType.DMA((taps,))],
        compiler_params=PARAMS,
        name="rows",
    )(pieces, other).reshape(weight.shape)

    out, grad = pl.pallas_call(
        join_kernel,
        out_shape=[jax.ShapeDtypeStruct((cells, width), bf16)] * 2,
        in_specs=[smem, *vmem(2)],
        out_specs=vmem(2),
        compiler_params=PARAMS,
        name="join",
    )(tile_counts, mine, tile_owner)
    return out.reshape(features.shape), grad.reshape(features.shape), grad_weight


def solution(mesh):
    return jax.shard_map(
        local,
        mesh=mesh,
        in_specs=(
            P("dp", "tile", None, None, None),
            P("dp", "tile", None, None, None),
            P(),
            P("dp", None),
            P("dp", None, None),
            P("dp"),
        ),
        out_specs=(P("dp", "tile", None, None, None), P("dp", "tile", None, None, None), P()),
        check_vma=False,
    )
```
